256 devices in a mesh: ctx: 32 (over x, z_hi, core), tp: 8 (over y, z_lo).
Axes of the slice: x: 4, y: 4, z: 8 (z_hi: 4, z_lo: 2; z = z_hi * 2 + z_lo), core: 2. Of those that a mesh axis runs over, the one named last changes fastest.
Arguments:
- query_branch: bfloat16 [16384, 4096], P('ctx', 'tp'), may hold values from -6 to 6
- key_branch: bfloat16 [16384, 4096], P('ctx', 'tp'), may hold values from 0 to 2
- value_branch: bfloat16 [16384, 4096], P('ctx', 'tp'), may hold values from 0 to 2
- filters: bfloat16 [16384, 4096], P('ctx', 'tp'), may hold values from -1.1 to 1.1
- skip_gain: float32 [4096], P('tp'), may hold values from -1 to 1
- out_weight: bfloat16 [4096, 4096], P('tp'), may hold values from -0.09375 to 0.09375
Outputs:
- mixed: bfloat16 [16384, 4096], P('ctx')
The draws below stay inside these ranges and needn't reach their ends.
All inputs are finite; a program needn't handle non-finite values.
Results may differ from the reference program's by a relative error of at most 0.018.
Values may be sent and summed in bfloat16 or wider, within the bound.
No kernel may reach another device: no remote copies, remote signals or barrier semaphores. Data moves between devices by JAX's collectives and lax.ppermute only.
A program may use at most 64 MiB of HBM per device.

```python
import math
import jax
import jax.numpy as jnp
from jax import lax

D = 4096
L_DEV = 512
LENGTH = 16384
BLOCKS = 64
FFT_LEN = 32768
GROUPS = 8
CH_GROUP = 512


def draw_filters(key, part):
    keys = jax.random.split(key, 7)
    sequence_position = jnp.arange(LENGTH, dtype=jnp.float32)[:, None]
    slow_rate = jnp.exp(jax.random.uniform(keys[0], (D,), jnp.float32, math.log(0.2 / LENGTH), math.log(2.0 / LENGTH)))
    fast_rate = jnp.exp(jax.random.uniform(keys[1], (D,), jnp.float32, math.log(1.0 / 50.0), math.log(1.0 / 30.0)))
    slow_share = 0.5
    chooser = jax.random.uniform(keys[2], (D,), jnp.float32)
    rate = jnp.where(chooser < slow_share, slow_rate, fast_rate)
    decay_envelope = jnp.exp(-rate[None, :] * sequence_position)
    delay_lags = jax.random.randint(keys[3], (3, D), 1, LENGTH).astype(jnp.float32)
    decay_drops = jax.random.uniform(keys[4], (3, D), jnp.float32, 0.5, 0.8)
    for pulse_index in range(3):
        decay_envelope = decay_envelope * jnp.where(sequence_position >= delay_lags[pulse_index][None, :], decay_drops[pulse_index][None, :], 1.0)
    scaling = jnp.sqrt(2.0 * rate / (1.0 - jnp.exp(-2.0 * rate * LENGTH)))
    noise = jnp.clip(jax.random.normal(keys[6], (LENGTH, D), jnp.float32), -4.0, 4.0)
    floor_level = 0.6 / LENGTH
    return (decay_envelope * scaling[None, :] * noise + floor_level).astype(jnp.bfloat16)


def level_of(stream_key, extent, cuts, low, largest):
    loudness = 1.0
    for position, blocks in cuts:
        steps = jax.random.uniform(jax.random.fold_in(jax.random.fold_in(stream_key, 6), position), (blocks,), jnp.float32, low / len(cuts), largest / len(cuts))
        loudness = loudness * jnp.repeat(jnp.exp(steps), extent[position] // blocks).reshape((-1,) + (1,) * (len(extent) - 1 - position))
    return loudness


def scatter_about(rng, extent, spread, limit, cuts=(), held_as=jnp.bfloat16):
    values = jax.random.normal(rng, extent, jnp.float32) * spread
    if len(cuts) > 0:
        values = level_of(rng, extent, cuts, -0.22, 0.18) * values
    return jnp.clip(values, min=-limit, max=limit).astype(held_as)


def setup_inputs(seed: int = 0) -> dict:
    streams_of = jax.random.split(jax.random.key(seed), 7)
    query_branch = scatter_about(streams_of[0], (LENGTH, D), 1.0, 6.0, ((0, 32), (1, 8)))
    key_branch = jnp.clip(2.0 * jax.random.uniform(streams_of[1], (LENGTH, D), jnp.float32) ** level_of(streams_of[1], (LENGTH, D), ((0, 32), (1, 8)), -0.2, 0.2), 0.0, 2.0).astype(jnp.bfloat16)
    value_branch = jnp.clip(2.0 * jax.random.uniform(streams_of[2], (LENGTH, D), jnp.float32) ** level_of(streams_of[2], (LENGTH, D), ((0, 32), (1, 8)), -0.2, 0.2), 0.0, 2.0).astype(jnp.bfloat16)
    filters = draw_filters(jax.random.fold_in(streams_of[6], 71), 0)
    skip_gain = jnp.clip(jax.random.uniform(streams_of[4], (D,), jnp.float32, -1.0, 1.0) * level_of(streams_of[4], (D,), ((0, 8),), -0.4, 0.0), -1.0, 1.0)
    out_weight = scatter_about(streams_of[5], (D, D), D ** -0.5, 0.09375, ((0, 8),))
    return {"query_branch": query_branch, "key_branch": key_branch, "value_branch": value_branch, "filters": filters, "skip_gain": skip_gain, "out_weight": out_weight}


def cosine_lookup_table(period, row_count, column_count, row_start, column_start):
    row_index = jnp.arange(row_count, dtype=jnp.int32) + row_start
    column_number_index = jnp.arange(column_count, dtype=jnp.int32) + column_start
    phase = (row_index[:, None] * column_number_index[None, :]) % period
    angle = phase.astype(jnp.float32) * (2.0 * math.pi / period)
    return jnp.cos(angle), jnp.sin(angle)


def round_half(value):
    return lax.optimization_barrier(value.astype(jnp.bfloat16))


def reference(query_branch, key_branch, value_branch, filters, skip_gain, out_weight):
    half_blocks = BLOCKS // 2
    mixer = round_half(key_branch.astype(jnp.float32) * value_branch.astype(jnp.float32))
    block_cos, block_sin = cosine_lookup_table(BLOCKS, BLOCKS, half_blocks, 0, 0)
    block_cos = block_cos.astype(jnp.bfloat16)
    block_sin = block_sin.astype(jnp.bfloat16)
    back_cos, back_sin = cosine_lookup_table(BLOCKS, half_blocks, BLOCKS, 0, 0)
    back_cos = back_cos.astype(jnp.bfloat16)
    back_sin = back_sin.astype(jnp.bfloat16)
    line_cos, line_sin = cosine_lookup_table(L_DEV, L_DEV, L_DEV, 0, 0)
    line_cos = line_cos.astype(jnp.bfloat16)
    line_sin = line_sin.astype(jnp.bfloat16)
    twist_cos, twist_sin = cosine_lookup_table(FFT_LEN, L_DEV, BLOCKS, 0, 0)
    twist_first_cos = jnp.transpose(twist_cos)[:, :, None]
    twist_first_sin = jnp.transpose(twist_sin)[:, :, None]
    twist_back_cos = twist_cos[:, :, None]
    twist_back_sin = twist_sin[:, :, None]

    def forward(signal):
        flat_rows = signal.reshape(half_blocks, L_DEV * CH_GROUP)
        real_part = jnp.dot(block_cos, flat_rows, preferred_element_type=jnp.float32).reshape(BLOCKS, L_DEV, CH_GROUP)
        imag_part = -jnp.dot(block_sin, flat_rows, preferred_element_type=jnp.float32).reshape(BLOCKS, L_DEV, CH_GROUP)
        first_real = round_half(real_part * twist_first_cos + imag_part * twist_first_sin)
        first_imag = round_half(imag_part * twist_first_cos - real_part * twist_first_sin)
        left_real = jnp.transpose(first_real, (1, 0, 2)).reshape(L_DEV, BLOCKS * CH_GROUP)
        left_imag = jnp.transpose(first_imag, (1, 0, 2)).reshape(L_DEV, BLOCKS * CH_GROUP)
        spec_real = jnp.dot(line_cos, left_real, preferred_element_type=jnp.float32) + jnp.dot(line_sin, left_imag, preferred_element_type=jnp.float32)
        spec_imag = jnp.dot(line_cos, left_imag, preferred_element_type=jnp.float32) - jnp.dot(line_sin, left_real, preferred_element_type=jnp.float32)
        return spec_real, spec_imag

    def group_output(running, inputs):
        query_group, mixer_group, filter_group, gain_group, weight_group = inputs
        mixer_real, mixer_imag = forward(mixer_group)
        filter_real, filter_imag = forward(filter_group)
        inverse_len = 1.0 / FFT_LEN
        prod_real = round_half((mixer_real * filter_real - mixer_imag * filter_imag) * inverse_len)
        prod_imag = round_half((mixer_real * filter_imag + mixer_imag * filter_real) * inverse_len)
        back_real = jnp.dot(line_cos, prod_real, preferred_element_type=jnp.float32) - jnp.dot(line_sin, prod_imag, preferred_element_type=jnp.float32)
        back_imag = jnp.dot(line_cos, prod_imag, preferred_element_type=jnp.float32) + jnp.dot(line_sin, prod_real, preferred_element_type=jnp.float32)
        back_real = back_real.reshape(L_DEV, BLOCKS, CH_GROUP)
        back_imag = back_imag.reshape(L_DEV, BLOCKS, CH_GROUP)
        second_real = round_half(back_real * twist_back_cos - back_imag * twist_back_sin)
        second_imag = round_half(back_imag * twist_back_cos + back_real * twist_back_sin)
        flat_real = jnp.transpose(second_real, (1, 0, 2)).reshape(BLOCKS, L_DEV * CH_GROUP)
        flat_imag = jnp.transpose(second_imag, (1, 0, 2)).reshape(BLOCKS, L_DEV * CH_GROUP)
        conv = jnp.dot(back_cos, flat_real, preferred_element_type=jnp.float32) - jnp.dot(back_sin, flat_imag, preferred_element_type=jnp.float32)
        conv = round_half(conv).reshape(LENGTH, CH_GROUP)
        gated = (query_group.astype(jnp.float32) * (conv.astype(jnp.float32) + gain_group[None, :] * mixer_group.astype(jnp.float32))).astype(jnp.bfloat16)
        partial_value = round_half(jnp.dot(gated, weight_group, preferred_element_type=jnp.float32))
        return running + partial_value.astype(jnp.float32), None

    def by_group(array):
        return jnp.transpose(array.reshape(LENGTH, GROUPS, CH_GROUP), (1, 0, 2))

    inputs = (by_group(query_branch), by_group(mixer), by_group(filters), skip_gain.reshape(GROUPS, CH_GROUP), out_weight.reshape(GROUPS, CH_GROUP, D))
    total, _ = lax.scan(group_output, jnp.zeros((LENGTH, D), jnp.float32), inputs)
    return total.astype(jnp.bfloat16)
```

```python
import math

import jax
import jax.numpy as jnp
import ml_dtypes
import numpy as np
from jax import lax
from jax.experimental import pallas as pl
from jax.experimental.pallas import tpu as pltpu
from jax.sharding import PartitionSpec as P

VMEM_BYTES = 40 * 1024 * 1024
GROUP = 4


def transform_tables(rows):
    j = np.arange(rows, dtype=np.int64)[:, None]
    f = np.arange(rows, dtype=np.int64)[None, :]
    angle = (j * (2 * f + 1) % (4 * rows)) * (2.0 * math.pi / (4 * rows))
    cos, sin = np.cos(angle), np.sin(angle)
    forward = np.concatenate([cos, -sin], 1)
    inverse = np.concatenate([cos.T, -sin.T], 0) / rows
    return forward.astype(ml_dtypes.bfloat16), inverse.astype(ml_dtypes.bfloat16)


def pack_kernel(key_ref, value_ref, filter_ref, out_ref):
    parts, both, rows = out_ref.shape
    share = both // 2
    mixer = key_ref[...].astype(jnp.float32) * value_ref[...].astype(jnp.float32)
    out_ref[:, :share, :] = mixer.astype(jnp.bfloat16).T.reshape(parts, share, rows)
    out_ref[:, share:, :] = filter_ref[...].T.reshape(parts, share, rows)


def conv_kernel(signal_ref, forward_ref, inverse_ref, out_ref, mixer_spec, filter_spec, product):
    blocks, both, rows = signal_ref.shape
    share = both // 2
    forward = forward_ref[...]

    def spectrum(signal):
        flat = signal.reshape(blocks * share, rows)
        value = jnp.dot(flat, forward, preferred_element_type=jnp.float32)
        return value.reshape(blocks, share, 2 * rows)

    mixer_spec[...] = spectrum(signal_ref[:, :share, :])
    filter_spec[...] = spectrum(signal_ref[:, share:, :])

    lane = lax.broadcasted_iota(jnp.int32, (8, 128), 1)
    sign = jnp.where(lane % 2 == 0, 1.0, -1.0).astype(jnp.float32)
    lane_tiles = rows // 128

    def tile(step, carry):
        row = pl.multiple_of((step // lane_tiles) * 8, 8)
        real = pl.multiple_of((step % lane_tiles) * 128, 128)
        imag = pl.multiple_of(rows + (step % lane_tiles) * 128, 128)

        def load(ref, block):
            return (
                ref[block, pl.ds(row, 8), pl.ds(real, 128)],
                ref[block, pl.ds(row, 8), pl.ds(imag, 128)],
            )

        def window(block):
            now_real, now_imag = load(mixer_spec, block)
            if block > 0:
                last_real, last_imag = load(mixer_spec, block - 1)
                now_real, now_imag = now_real - sign * last_imag, now_imag + sign * last_real
            return now_real, now_imag

        for block in reversed(range(blocks)):
            now_real, now_imag = window(block)
            mixer_spec[block, pl.ds(row, 8), pl.ds(real, 128)] = now_real
            mixer_spec[block, pl.ds(row, 8), pl.ds(imag, 128)] = now_imag

        for first in range(0, blocks, GROUP):
            sums = [[None] * 3 for _ in range(GROUP)]
            held = {}
            for lag in range(first + GROUP):
                filter_real, filter_imag = load(filter_spec, lag)
                filter_both = filter_real + filter_imag
                for i in range(GROUP):
                    block = first + i - lag
                    if block < 0:
                        continue
                    if block not in held:
                        real_part, imag_part = load(mixer_spec, block)
                        held[block] = (real_part, imag_part, real_part + imag_part)
                    terms = (
                        filter_real * held[block][0],
                        filter_imag * held[block][1],
                        filter_both * held[block][2],
                    )
                    for s in range(3):
                        sums[i][s] = terms[s] if sums[i][s] is None else sums[i][s] + terms[s]
                held.pop(first + GROUP - 1 - lag, None)
            for i in range(GROUP):
                one, two, three = sums[i]
                product[first + i, pl.ds(row, 8), pl.ds(real, 128)] = one - two
                product[first + i, pl.ds(row, 8), pl.ds(imag, 128)] = three - one - two
        return carry

    lax.fori_loop(0, (share // 8) * lane_tiles, tile, 0)
    flat = product[...].astype(jnp.bfloat16).reshape(blocks * share, 2 * rows)
    conv = jnp.dot(flat, inverse_ref[...], preferred_element_type=jnp.float32)
    out_ref[...] = conv.astype(jnp.bfloat16).reshape(blocks, share, rows)


def project_kernel(conv_ref, query_ref, key_ref, value_ref, gain_ref, weight_ref, out_ref):
    rows, channels = query_ref.shape
    conv = conv_ref[...].reshape(channels, rows).T.astype(jnp.float32)
    mixer = key_ref[...].astype(jnp.float32) * value_ref[...].astype(jnp.float32)
    mixer = mixer.astype(jnp.bfloat16).astype(jnp.float32)
    gated = query_ref[...].astype(jnp.float32) * (conv + gain_ref[...] * mixer)
    gated = gated.astype(jnp.bfloat16)
    width = 1024
    for start in range(0, out_ref.shape[1], width):
        value = jnp.dot(
            gated, weight_ref[:, start : start + width], preferred_element_type=jnp.float32
        )
        out_ref[:, start : start + width] = value.astype(jnp.bfloat16)


def whole(kernel, out_shape, scratch=()):
    return pl.pallas_call(
        kernel,
        out_shape=jax.ShapeDtypeStruct(out_shape, jnp.bfloat16),
        scratch_shapes=list(scratch),
        compiler_params=pltpu.CompilerParams(vmem_limit_bytes=VMEM_BYTES),
    )


def body(query_branch, key_branch, value_branch, filters, skip_gain, out_weight):
    ctx_count = lax.axis_size("ctx")
    rows, channels = query_branch.shape
    share = channels // ctx_count
    forward, inverse = (jnp.asarray(table) for table in transform_tables(rows))

    with jax.named_scope("pack"):
        outgoing = whole(pack_kernel, (ctx_count, 2 * share, rows))(
            key_branch, value_branch, filters
        )
    arrived = lax.all_to_all(outgoing, "ctx", split_axis=0, concat_axis=0, tiled=True)
    spec = pltpu.VMEM((ctx_count, share, 2 * rows), jnp.float32)
    with jax.named_scope("conv"):
        conv = whole(conv_kernel, (ctx_count, share, rows), (spec, spec, spec))(
            arrived, forward, inverse
        )
    conv = lax.all_to_all(conv, "ctx", split_axis=0, concat_axis=0, tiled=True)
    with jax.named_scope("project"):
        partial_value = whole(project_kernel, (rows, out_weight.shape[1]))(
            conv, query_branch, key_branch, value_branch, skip_gain[None, :], out_weight
        )
    tp_count = lax.axis_size("tp")
    pieces = lax.all_to_all(partial_value, "tp", split_axis=0, concat_axis=0, tiled=True)
    pieces = pieces.reshape(tp_count, rows // tp_count, -1)
    summed = pieces.astype(jnp.float32).sum(0).astype(jnp.bfloat16)
    return lax.all_gather(summed, "tp", axis=0, tiled=True)


def solution(mesh):
    placed = (
        P("ctx", "tp"),
        P("ctx", "tp"),
        P("ctx", "tp"),
        P("ctx", "tp"),
        P("tp"),
        P("tp", None),
    )
    return jax.shard_map(
        body, mesh=mesh, in_specs=placed, out_specs=P("ctx", None), check_vma=False
    )
```

```python
import math

import jax
import jax.numpy as jnp
import ml_dtypes
import numpy as np
from jax import lax
from jax.experimental import pallas as pl
from jax.experimental.pallas import tpu as pltpu
from jax.sharding import PartitionSpec as P

VMEM_BYTES = 24 * 1024 * 1024
GROUP = 4
TP = 8
CUTS = (0, 1408, 2688, 4096)
ALONG_Z = [(i, i ^ 1) for i in range(TP)]
UP_Y = [(i, (i + 2) % TP) for i in range(TP)]
DOWN_Y = [(i, (i - 2) % TP) for i in range(TP)]


def transform_tables(rows):
    j = np.arange(rows, dtype=np.int64)[:, None]
    f = np.arange(rows, dtype=np.int64)[None, :]
    angle = (j * (2 * f + 1) % (4 * rows)) * (2.0 * math.pi / (4 * rows))
    cos, sin = np.cos(angle), np.sin(angle)
    forward = np.concatenate([cos, -sin], 1)
    inverse = np.concatenate([cos.T, -sin.T], 0) / rows
    return forward.astype(ml_dtypes.bfloat16), inverse.astype(ml_dtypes.bfloat16)


def pack_kernel(key_ref, value_ref, filter_ref, out_ref):
    parts, both, rows = out_ref.shape
    share = both // 2
    mixer = key_ref[...].astype(jnp.float32) * value_ref[...].astype(jnp.float32)
    out_ref[:, :share, :] = mixer.astype(jnp.bfloat16).T.reshape(parts, share, rows)
    out_ref[:, share:, :] = filter_ref[...].T.reshape(parts, share, rows)


def conv_kernel(signal_ref, forward_ref, inverse_ref, out_ref, mixer_spec, filter_spec, product):
    blocks, both, rows = signal_ref.shape
    share = both // 2
    forward = forward_ref[...]

    def spectrum(signal):
        flat = signal.reshape(blocks * share, rows)
        value = jnp.dot(flat, forward, preferred_element_type=jnp.float32)
        return value.reshape(blocks, share, 2 * rows)

    mixer_spec[...] = spectrum(signal_ref[:, :share, :])
    filter_spec[...] = spectrum(signal_ref[:, share:, :])

    lane = lax.broadcasted_iota(jnp.int32, (8, 128), 1)
    sign = jnp.where(lane % 2 == 0, 1.0, -1.0).astype(jnp.float32)
    lane_tiles = rows // 128

    def tile(step, carry):
        row = pl.multiple_of((step // lane_tiles) * 8, 8)
        real = pl.multiple_of((step % lane_tiles) * 128, 128)
        imag = pl.multiple_of(rows + (step % lane_tiles) * 128, 128)

        def load(ref, block):
            return (
                ref[block, pl.ds(row, 8), pl.ds(real, 128)],
                ref[block, pl.ds(row, 8), pl.ds(imag, 128)],
            )

        def window(block):
            now_real, now_imag = load(mixer_spec, block)
            if block > 0:
                last_real, last_imag = load(mixer_spec, block - 1)
                now_real, now_imag = now_real - sign * last_imag, now_imag + sign * last_real
            return now_real, now_imag

        for block in reversed(range(blocks)):
            now_real, now_imag = window(block)
            mixer_spec[block, pl.ds(row, 8), pl.ds(real, 128)] = now_real
            mixer_spec[block, pl.ds(row, 8), pl.ds(imag, 128)] = now_imag

        for first in range(0, blocks, GROUP):
            sums = [[None] * 3 for _ in range(GROUP)]
            held = {}
            for lag in range(first + GROUP):
                filter_real, filter_imag = load(filter_spec, lag)
                filter_both = filter_real + filter_imag
                for i in range(GROUP):
                    block = first + i - lag
                    if block < 0:
                        continue
                    if block not in held:
                        real_part, imag_part = load(mixer_spec, block)
                        held[block] = (real_part, imag_part, real_part + imag_part)
                    terms = (
                        filter_real * held[block][0],
                        filter_imag * held[block][1],
                        filter_both * held[block][2],
                    )
                    for s in range(3):
                        sums[i][s] = terms[s] if sums[i][s] is None else sums[i][s] + terms[s]
                held.pop(first + GROUP - 1 - lag, None)
            for i in range(GROUP):
                one, two, three = sums[i]
                product[first + i, pl.ds(row, 8), pl.ds(real, 128)] = one - two
                product[first + i, pl.ds(row, 8), pl.ds(imag, 128)] = three - one - two
        return carry

    lax.fori_loop(0, (share // 8) * lane_tiles, tile, 0)
    flat = product[...].astype(jnp.bfloat16).reshape(blocks * share, 2 * rows)
    conv = jnp.dot(flat, inverse_ref[...], preferred_element_type=jnp.float32)
    out_ref[...] = conv.astype(jnp.bfloat16).reshape(blocks, share, rows)


def project_kernel(
    order_ref, conv_ref, query_ref, key_ref, value_ref, gain_ref, weight_ref, *refs
):
    outs, (conv_rows, gated_rows) = refs[:-2], refs[-2:]
    rows, channels = query_ref.shape
    conv_rows[...] = conv_ref[...].reshape(channels, rows).T
    piece = rows // TP
    for slot in range(TP):
        here = pl.ds(pl.multiple_of(order_ref[slot] * piece, piece), piece)
        mixer = key_ref[here, :].astype(jnp.float32) * value_ref[here, :].astype(jnp.float32)
        mixer = mixer.astype(jnp.bfloat16).astype(jnp.float32)
        total = conv_rows[here, :].astype(jnp.float32) + gain_ref[...] * mixer
        gated = query_ref[here, :].astype(jnp.float32) * total
        gated_rows[slot * piece : (slot + 1) * piece, :] = gated.astype(jnp.bfloat16)
    gated = gated_rows[...]
    for cut, start in enumerate(CUTS[:-1]):
        columns = slice(start, CUTS[cut + 1])
        value = jnp.dot(gated, weight_ref[:, columns], preferred_element_type=jnp.float32)
        value = value.astype(jnp.bfloat16)
        for slot in range(TP):
            outs[slot][:, columns] = value[slot * piece : (slot + 1) * piece]


def whole(kernel, shapes, scratch=(), scalars=0, operands=0):
    several = isinstance(shapes, list)
    out = [jax.ShapeDtypeStruct(shape, jnp.bfloat16) for shape in (shapes if several else [shapes])]
    specs = {}
    if scalars:
        specs["in_specs"] = [pl.BlockSpec(memory_space=pltpu.SMEM)] * scalars + [
            pl.BlockSpec(memory_space=pltpu.VMEM)
        ] * operands
    return pl.pallas_call(
        kernel,
        out_shape=out if several else out[0],
        scratch_shapes=list(scratch),
        compiler_params=pltpu.CompilerParams(vmem_limit_bytes=VMEM_BYTES),
        **specs,
    )


def along_z(value):
    return lax.ppermute(value, "tp", ALONG_Z)


def up_y(value):
    return lax.ppermute(value, "tp", UP_Y)


def down_y(value):
    return lax.ppermute(value, "tp", DOWN_Y)


def add(*terms):
    return sum(term.astype(jnp.float32) for term in terms).astype(jnp.bfloat16)


def add_part(whole_value, part, cut):
    first, last = CUTS[cut], CUTS[cut + 1]
    return jnp.concatenate(
        [whole_value[:, :first], add(whole_value[:, first:last], part), whole_value[:, last:]], 1
    )


def reduce_pieces(own, own_z, up, up_z, far, far_z, down, down_z):
    first = far_z[:, CUTS[0] : CUTS[1]], far_z[:, CUTS[1] : CUTS[2]], far_z[:, CUTS[2] : CUTS[3]]
    far = add_part(far, along_z(first[0]), 0)
    down_z = add_part(down_z, down_y(first[1]), 1)
    up_z = add_part(up_z, up_y(first[2]), 2)
    from_z, from_up, from_down = along_z(up_z), down_y(down_z), up_y(far)
    from_up, down = lax.optimization_barrier((from_up, down))
    up = add(up, from_z, from_down)
    own_z = add(own_z, from_up)
    return add(own, along_z(own_z), up_y(up), down_y(down))


def gather_pieces(own, order):
    own_z, down, up = along_z(own), up_y(own), down_y(own)
    up_z, down_z, far = along_z(up), up_y(own_z), down_y(up)
    far_z = jnp.concatenate(
        [
            along_z(far[:, CUTS[0] : CUTS[1]]),
            up_y(down_z[:, CUTS[1] : CUTS[2]]),
            down_y(up_z[:, CUTS[2] : CUTS[3]]),
        ],
        1,
    )
    piece, columns = own.shape
    out = jnp.zeros((TP * piece, columns), own.dtype)
    for slot, value in enumerate((own, own_z, up, up_z, far, far_z, down, down_z)):
        out = lax.dynamic_update_slice(out, value, (order[slot] * piece, 0))
    return out


def body(query_branch, key_branch, value_branch, filters, skip_gain, out_weight):
    ctx_count = lax.axis_size("ctx")
    rows, channels = query_branch.shape
    share = channels // ctx_count
    forward, inverse = (jnp.asarray(table) for table in transform_tables(rows))

    with jax.named_scope("pack"):
        outgoing = whole(pack_kernel, (ctx_count, 2 * share, rows))(
            key_branch, value_branch, filters
        )
    arrived = lax.all_to_all(outgoing, "ctx", split_axis=0, concat_axis=0, tiled=True)
    spec = pltpu.VMEM((ctx_count, share, 2 * rows), jnp.float32)
    with jax.named_scope("conv"):
        conv = whole(conv_kernel, (ctx_count, share, rows), (spec, spec, spec))(
            arrived, forward, inverse
        )
    conv = lax.all_to_all(conv, "ctx", split_axis=0, concat_axis=0, tiled=True)
    place = lax.axis_index("tp")
    slots = jnp.arange(TP, dtype=jnp.int32)
    order = (place // 2 + slots // 2) % (TP // 2) * 2 + (place + slots) % 2
    piece = rows // TP
    with jax.named_scope("project"):
        pieces = whole(
            project_kernel,
            [(piece, out_weight.shape[1])] * TP,
            (pltpu.VMEM((rows, channels), jnp.bfloat16), pltpu.VMEM((rows, channels), jnp.bfloat16)),
            scalars=1,
            operands=6,
        )(order, conv, query_branch, key_branch, value_branch, skip_gain[None, :], out_weight)
    with jax.named_scope("reduce"):
        summed = reduce_pieces(*pieces)
    with jax.named_scope("gather"):
        return gather_pieces(summed, order)


def solution(mesh):
    placed = (
        P("ctx", "tp"),
        P("ctx", "tp"),
        P("ctx", "tp"),
        P("ctx", "tp"),
        P("tp"),
        P("tp", None),
    )
    return jax.shard_map(
        body, mesh=mesh, in_specs=placed, out_specs=P("ctx", None), check_vma=False
    )
```

```python
import functools
import math

import jax
import jax.numpy as jnp
import ml_dtypes
import numpy as np
from jax import lax
from jax.experimental import pallas as pl
from jax.experimental.pallas import tpu as pltpu
from jax.sharding import Mesh, PartitionSpec as P

MIB = 1024 * 1024
GROUP = 4
CUTS = (0, 1408, 2688, 4096)
CTX_Y = ("block", "core", "y")


def transform_tables(rows):
    j = np.arange(rows, dtype=np.int64)[:, None]
    f = np.arange(rows, dtype=np.int64)[None, :]
    angle = (j * (2 * f + 1) % (4 * rows)) * (2.0 * math.pi / (4 * rows))
    cos, sin = np.cos(angle), np.sin(angle)
    forward = np.concatenate([cos, -sin], 1)
    inverse = np.concatenate([cos.T, -sin.T], 0) / rows
    return forward.astype(ml_dtypes.bfloat16), inverse.astype(ml_dtypes.bfloat16)


def pack_kernel(
    key_hbm, value_hbm, filter_hbm, query_hbm, weight_hbm,
    out_ref, half_hbm, up_hbm, down_hbm, far_hbm, key_ref, value_ref, filter_ref, sems,
):
    parts, both, rows = out_ref.shape
    share = both // 2
    half, quarter = half_hbm.shape[0], up_hbm.shape[0]

    core, y = lax.axis_index("core"), lax.axis_index("y")

    def rows_of(ref, index, count):
        return ref.at[pl.ds(pl.multiple_of(index * count, count), count)]

    copies = [
        pltpu.make_async_copy(source, target, sems.at[i])
        for i, (source, target) in enumerate(
            (
                (key_hbm, key_ref),
                (value_hbm, value_ref),
                (filter_hbm, filter_ref),
                (rows_of(weight_hbm, core, half), half_hbm),
                (rows_of(query_hbm, (y + 1) % 4, quarter), up_hbm),
                (rows_of(query_hbm, (y + 3) % 4, quarter), down_hbm),
                (rows_of(query_hbm, (y + 2) % 4, quarter), far_hbm),
            )
        )
    ]
    for copy in copies:
        copy.start()
    copies[0].wait()
    copies[1].wait()
    mixer = key_ref[...].astype(jnp.float32) * value_ref[...].astype(jnp.float32)
    out_ref[:, :share, :] = mixer.astype(jnp.bfloat16).T.reshape(parts, share, rows)
    copies[2].wait()
    out_ref[:, share:, :] = filter_ref[...].T.reshape(parts, share, rows)
    for copy in copies[3:]:
        copy.wait()


def conv_kernel(
    signal_ref, gain_ref, forward_ref, inverse_ref, out_ref, mixer_spec, filter_spec, product
):
    blocks, both, rows = signal_ref.shape
    share = both // 2
    forward = forward_ref[...]

    def spectrum(signal):
        flat = signal.reshape(blocks * share, rows)
        value = jnp.dot(flat, forward, preferred_element_type=jnp.float32)
        return value.reshape(blocks, share, 2 * rows)

    mixer_spec[...] = spectrum(signal_ref[:, :share, :])
    filter_spec[...] = spectrum(signal_ref[:, share:, :])

    lane = lax.broadcasted_iota(jnp.int32, (8, 128), 1)
    sign = jnp.where(lane % 2 == 0, 1.0, -1.0).astype(jnp.float32)
    lane_tiles = rows // 128

    def tile(step, carry):
        row = pl.multiple_of((step // lane_tiles) * 8, 8)
        real = pl.multiple_of((step % lane_tiles) * 128, 128)
        imag = pl.multiple_of(rows + (step % lane_tiles) * 128, 128)

        def load(ref, block):
            return (
                ref[block, pl.ds(row, 8), pl.ds(real, 128)],
                ref[block, pl.ds(row, 8), pl.ds(imag, 128)],
            )

        def window(block):
            now_real, now_imag = load(mixer_spec, block)
            if block > 0:
                last_real, last_imag = load(mixer_spec, block - 1)
                now_real, now_imag = now_real - sign * last_imag, now_imag + sign * last_real
            return now_real, now_imag

        for block in reversed(range(blocks)):
            now_real, now_imag = window(block)
            mixer_spec[block, pl.ds(row, 8), pl.ds(real, 128)] = now_real
            mixer_spec[block, pl.ds(row, 8), pl.ds(imag, 128)] = now_imag

        for first in range(0, blocks, GROUP):
            sums = [[None] * 3 for _ in range(GROUP)]
            held = {}
            for lag in range(first + GROUP):
                filter_real, filter_imag = load(filter_spec, lag)
                filter_both = filter_real + filter_imag
                for i in range(GROUP):
                    block = first + i - lag
                    if block < 0:
                        continue
                    if block not in held:
                        real_part, imag_part = load(mixer_spec, block)
                        held[block] = (real_part, imag_part, real_part + imag_part)
                    terms = (
                        filter_real * held[block][0],
                        filter_imag * held[block][1],
                        filter_both * held[block][2],
                    )
                    for s in range(3):
                        sums[i][s] = terms[s] if sums[i][s] is None else sums[i][s] + terms[s]
                held.pop(first + GROUP - 1 - lag, None)
            for i in range(GROUP):
                one, two, three = sums[i]
                product[first + i, pl.ds(row, 8), pl.ds(real, 128)] = one - two
                product[first + i, pl.ds(row, 8), pl.ds(imag, 128)] = three - one - two
        return carry

    lax.fori_loop(0, (share // 8) * lane_tiles, tile, 0)
    flat = product[...].astype(jnp.bfloat16).reshape(blocks * share, 2 * rows)
    conv = jnp.dot(flat, inverse_ref[...], preferred_element_type=jnp.float32)
    mixer = signal_ref[:, :share, :].astype(jnp.float32)
    total = (conv.reshape(blocks, share, rows) + gain_ref[...] * mixer).astype(jnp.bfloat16)
    quarters, width = out_ref.shape[1], out_ref.shape[3]
    for quarter in range(quarters):
        out_ref[:, quarter] = total[:, :, quarter * width : (quarter + 1) * width]


def gate(total_ref, query_ref, up_ref, down_ref, far_ref, out_ref, gated_ref):
    blocks, groups, share, rows = total_ref.shape
    half = blocks * share // 2
    core, y, keep = lax.axis_index("core"), lax.axis_index("y"), lax.axis_index("z")
    own = query_ref.at[pl.ds(pl.multiple_of(y * rows, rows), rows)]
    sources = (own, y), (up_ref, (y + 3) % 4), (down_ref, (y + 1) % 4), (far_ref, (y + 2) % 4)
    for group, (query, source) in enumerate(sources):
        for part in range(2):
            side = part if group == 0 else (core if part == 0 else 1 - core)
            total = total_ref[pl.ds(side * (blocks // 2), blocks // 2), source]
            total = total.reshape(half, rows).T.astype(jnp.float32)
            channels = side * half if group == 0 else pl.multiple_of(side * half, half)
            value = query[:, pl.ds(channels, half)].astype(jnp.float32) * total
            start = (2 * group + part) * half
            gated_ref[:, start : start + half] = value.astype(jnp.bfloat16)
    piece = rows // 2
    out_ref[:piece] = gated_ref[pl.ds(pl.multiple_of((1 - keep) * piece, piece), piece), :]
    out_ref[piece:] = gated_ref[pl.ds(pl.multiple_of(keep * piece, piece), piece), :]


def project_kernel(first, prepare, *refs):
    count = 5 if prepare else 1
    weights, rest = refs[count : count + 9], refs[count + 9 :]
    if prepare:
        other_ref, own_ref, gated_ref, _, buffer, sems, rows_ref = rest
    else:
        gated_ref = refs[0]
        other_ref, own_ref, buffer, sems = rest
    piece, columns = other_ref.shape
    slots, _, width = buffer.shape
    steps = columns // width

    def copies(step):
        start, made = 0, []
        for i, weight in enumerate(weights):
            depth = weight.shape[0]
            source = weight.at[:, pl.ds(first + step * width, width)]
            target = buffer.at[step % slots, pl.ds(start, depth)]
            made.append(pltpu.make_async_copy(source, target, sems.at[step % slots, i]))
            start += depth
        return made

    for step in range(min(slots, steps)):
        for copy in copies(step):
            copy.start()
    if prepare:
        gate(*refs[:5], gated_ref, rows_ref)
    gated = gated_ref[...]
    for step in range(steps):
        for copy in copies(step):
            copy.wait()
        value = jnp.dot(gated, buffer[step % slots], preferred_element_type=jnp.float32)
        value = value.astype(jnp.bfloat16)
        other_ref[:, step * width : (step + 1) * width] = value[:piece]
        own_ref[:, step * width : (step + 1) * width] = value[piece:]
        if step + slots < steps:
            for copy in copies(step + slots):
                copy.start()


VMEM = pl.BlockSpec(memory_space=pltpu.VMEM)
HBM = pl.BlockSpec(memory_space=pltpu.HBM)


def whole(kernel, shapes, in_specs, out_specs, scratch=(), limit=16):
    return pl.pallas_call(
        kernel,
        out_shape=[jax.ShapeDtypeStruct(shape, jnp.bfloat16) for shape in shapes],
        in_specs=in_specs,
        out_specs=out_specs,
        scratch_shapes=list(scratch),
        compiler_params=pltpu.CompilerParams(vmem_limit_bytes=limit * MIB),
    )


def project(operands, weights, first, last, prepare, width=512, slots=3):
    features = last - first
    rows, depth = operands[0].shape[3] if prepare else operands[0].shape[0], 0
    depth = sum(weight.shape[0] for weight in weights)
    shapes = [(rows // 2, features)] * 2
    scratch = [
        pltpu.VMEM((slots, depth, width), jnp.bfloat16),
        pltpu.SemaphoreType.DMA((slots, len(weights))),
    ]
    if prepare:
        shapes += [(rows, depth), (rows * lax.axis_size("y"), features)]
        scratch.append(pltpu.VMEM((rows, depth), jnp.bfloat16))
    return whole(
        functools.partial(project_kernel, first, prepare),
        shapes,
        [VMEM] * len(operands) + [HBM] * len(weights),
        [VMEM] * 3 + [HBM] if prepare else [VMEM] * 2,
        scratch,
        limit=16,
    )(*operands, *weights)


def swap(axis):
    return lambda value: lax.ppermute(value, axis, [(0, 1), (1, 0)])


along_z, along_core = swap("z"), swap("core")


def along_y(value, steps):
    count = lax.axis_size("y")
    return lax.ppermute(value, "y", [(i, (i + steps) % count) for i in range(count)])


def add(*terms):
    return sum(term.astype(jnp.float32) for term in terms).astype(jnp.bfloat16)


def gather_pieces(own, order, out):
    own_z, down, up = along_z(own), along_y(own, 1), along_y(own, -1)
    up_z, down_z, far = along_z(up), along_y(own_z, 1), along_y(up, -1)
    far_z = jnp.concatenate(
        [
            along_z(far[:, CUTS[0] : CUTS[1]]),
            along_y(down_z[:, CUTS[1] : CUTS[2]], 1),
            along_y(up_z[:, CUTS[2] : CUTS[3]], -1),
        ],
        1,
    )
    for slot, value in enumerate((own, own_z, up, up_z, far, far_z, down, down_z)):
        out = lax.dynamic_update_slice(out, value, (order[slot] * own.shape[0], 0))
    return out


def body(query_branch, key_branch, value_branch, filters, skip_gain, out_weight):
    core, y, z = (lax.axis_index(name) for name in ("core", "y", "z"))
    ctx = lax.axis_index("block") * 2 + core
    ctx_count = lax.axis_size("block") * 2
    y_count = lax.axis_size("y")
    rows, channels = query_branch.shape
    share = channels // ctx_count
    features = out_weight.shape[1]
    quarter = rows // y_count
    forward, inverse = (jnp.asarray(table) for table in transform_tables(rows))
    gain = lax.dynamic_slice(skip_gain, (ctx * share,), (share,))[:, None]

    with jax.named_scope("pack"):
        square = pltpu.VMEM((rows, channels), jnp.bfloat16)
        outgoing, weight_half, to_up, to_down, to_far = whole(
            pack_kernel,
            [(ctx_count, 2 * share, rows), (channels // 2, features)] + [(quarter, channels)] * 3,
            [HBM] * 5,
            [VMEM] + [HBM] * 4,
            [square, square, square, pltpu.SemaphoreType.DMA((7,))],
            limit=60,
        )(key_branch, value_branch, filters, query_branch, out_weight)
    with jax.named_scope("weights"):
        weight_up, weight_down = along_y(weight_half, 1), along_y(weight_half, -1)
        query_up, query_down = along_y(to_up, 1), along_y(to_down, -1)
        query_far = along_y(to_far, 2)
    arrived = lax.all_to_all(outgoing, ("block", "core"), split_axis=0, concat_axis=0, tiled=True)
    spec = pltpu.VMEM((ctx_count, share, 2 * rows), jnp.float32)
    with jax.named_scope("conv"):
        (total,) = whole(
            conv_kernel,
            [(ctx_count, y_count, share, quarter)],
            [VMEM] * 4,
            [VMEM],
            [spec] * 3,
            limit=24,
        )(arrived, gain, forward, inverse)
    with jax.named_scope("weights"):
        total, weight_up, weight_down, query_up, query_down, query_far = lax.optimization_barrier(
            (total, weight_up, weight_down, query_up, query_down, query_far)
        )
        cut = channels // 4
        far_first, far_last = along_y(weight_up[:cut], 1), along_y(weight_down[cut:], -1)
        swapped_up, swapped_down = along_core(weight_up), along_core(weight_down)
    total = lax.all_to_all(
        total.reshape(ctx_count * y_count, share, quarter), CTX_Y, split_axis=0, concat_axis=0,
        tiled=True,
    ).reshape(ctx_count, y_count, share, quarter)
    with jax.named_scope("weights"):
        total, far_first, far_last = lax.optimization_barrier((total, far_first, far_last))
        swapped_first, swapped_last = along_core(far_first), along_core(far_last)
    weights = (
        out_weight, weight_up, swapped_up, weight_down, swapped_down,
        far_first, far_last, swapped_first, swapped_last,
    )
    with jax.named_scope("project"):
        operands = (total, query_branch, query_up, query_down, query_far)
        other, own, _, blank = project(operands, weights, 0, features, True)
    with jax.named_scope("reduce"):
        summed = add(own, along_z(other))
    slots = jnp.arange(2 * y_count, dtype=jnp.int32)
    order = (y + slots // 2) % y_count * 2 + (z + slots) % 2
    with jax.named_scope("gather"):
        return gather_pieces(summed, order, blank)


def solution(mesh):
    fine = Mesh(mesh.devices.reshape(-1, 2, 4, 2), ("block", "core", "y", "z"))
    ctx, tp = ("block", "core"), ("y", "z")
    placed = (P(ctx, tp), P(ctx, tp), P(ctx, tp), P(ctx, tp), P(tp), P(tp, None))
    return jax.shard_map(
        body, mesh=fine, in_specs=placed, out_specs=P(ctx, None), check_vma=False
    )
```

```python
import functools
import math

import jax
import jax.numpy as jnp
import ml_dtypes
import numpy as np
from jax import lax
from jax.experimental import pallas as pl
from jax.experimental.pallas import tpu as pltpu
from jax.sharding import Mesh, PartitionSpec as P

MIB = 1024 * 1024
GROUP = 4
STEPS = (0, 1, -1, 2)
STREAMS = 2
WIDTH = 512


def transform_tables(rows):
    j = np.arange(rows, dtype=np.int64)[:, None]
    f = np.arange(rows, dtype=np.int64)[None, :]
    angle = (j * (2 * f + 1) % (4 * rows)) * (2.0 * math.pi / (4 * rows))
    cos, sin = np.cos(angle), np.sin(angle)
    forward = np.concatenate([cos, -sin], 1)
    inverse = np.concatenate([cos.T, -sin.T], 0) / rows
    return forward.astype(ml_dtypes.bfloat16), inverse.astype(ml_dtypes.bfloat16)


def pack_kernel(
    key_hbm, value_hbm, filter_hbm, query_hbm, weight_hbm,
    out_ref, half_ref, up_ref, down_ref, far_ref, key_ref, value_ref, filter_ref, sems,
):
    parts, both, rows = out_ref.shape
    share = both // 2
    half, quarter = half_ref.shape[0], up_ref.shape[0]

    core, y = lax.axis_index("core"), lax.axis_index("y")

    def rows_of(ref, index, count):
        return ref.at[pl.ds(pl.multiple_of(index * count, count), count)]

    copies = [
        pltpu.make_async_copy(source, target, sems.at[i])
        for i, (source, target) in enumerate(
            (
                (key_hbm, key_ref),
                (value_hbm, value_ref),
                (filter_hbm, filter_ref),
                (rows_of(weight_hbm, core, half), half_ref),
                (rows_of(query_hbm, (y + 1) % 4, quarter), up_ref),
                (rows_of(query_hbm, (y + 3) % 4, quarter), down_ref),
                (rows_of(query_hbm, (y + 2) % 4, quarter), far_ref),
            )
        )
    ]
    for copy in copies:
        copy.start()
    copies[0].wait()
    copies[1].wait()
    mixer = key_ref[...].astype(jnp.float32) * value_ref[...].astype(jnp.float32)
    out_ref[:, :share, :] = mixer.astype(jnp.bfloat16).T.reshape(parts, share, rows)
    copies[2].wait()
    out_ref[:, share:, :] = filter_ref[...].T.reshape(parts, share, rows)
    for copy in copies[3:]:
        copy.wait()


def conv_kernel(
    signal_ref, gain_ref, forward_hbm, inverse_hbm, out_ref, mixer_spec, filter_spec, product,
    sum_ref, forward_ref, inverse_ref, sems,
):
    blocks, both, rows = signal_ref.shape
    share = both // 2
    copies = []
    for source, target in ((forward_hbm, forward_ref), (inverse_hbm, inverse_ref)):
        count = source.shape[0] // 4
        for part in range(4):
            here = pl.ds(part * count, count)
            copies.append(
                pltpu.make_async_copy(source.at[here], target.at[here], sems.at[len(copies)])
            )
    for copy in copies:
        copy.start()
    for copy in copies[:4]:
        copy.wait()
    forward = forward_ref[...]

    def spectrum(signal):
        flat = signal.reshape(blocks * share, rows)
        value = jnp.dot(flat, forward, preferred_element_type=jnp.float32)
        return value.reshape(blocks, share, 2 * rows)

    mixer_spec[...] = spectrum(signal_ref[:, :share, :])
    filter_spec[...] = spectrum(signal_ref[:, share:, :])

    lane = lax.broadcasted_iota(jnp.int32, (8, 128), 1)
    sign = jnp.where(lane % 2 == 0, 1.0, -1.0).astype(jnp.float32)
    lane_tiles = rows // 128

    def tile(step, carry):
        row = pl.multiple_of((step // lane_tiles) * 8, 8)
        real = pl.multiple_of((step % lane_tiles) * 128, 128)
        imag = pl.multiple_of(rows + (step % lane_tiles) * 128, 128)

        def load(ref, block):
            return (
                ref[block, pl.ds(row, 8), pl.ds(real, 128)],
                ref[block, pl.ds(row, 8), pl.ds(imag, 128)],
            )

        def window(block):
            now_real, now_imag = load(mixer_spec, block)
            if block > 0:
                last_real, last_imag = load(mixer_spec, block - 1)
                now_real, now_imag = now_real - sign * last_imag, now_imag + sign * last_real
            return now_real, now_imag

        for block in reversed(range(blocks)):
            now_real, now_imag = window(block)
            mixer_spec[block, pl.ds(row, 8), pl.ds(real, 128)] = now_real
            mixer_spec[block, pl.ds(row, 8), pl.ds(imag, 128)] = now_imag

        for first in range(0, blocks, GROUP):
            sums = [[None] * 3 for _ in range(GROUP)]
            held = {}
            for lag in range(first + GROUP):
                filter_real, filter_imag = load(filter_spec, lag)
                filter_both = filter_real + filter_imag
                for i in range(GROUP):
                    block = first + i - lag
                    if block < 0:
                        continue
                    if block not in held:
                        real_part, imag_part = load(mixer_spec, block)
                        held[block] = (real_part, imag_part, real_part + imag_part)
                    terms = (
                        filter_real * held[block][0],
                        filter_imag * held[block][1],
                        filter_both * held[block][2],
                    )
                    for s in range(3):
                        sums[i][s] = terms[s] if sums[i][s] is None else sums[i][s] + terms[s]
                held.pop(first + GROUP - 1 - lag, None)
            for i in range(GROUP):
                one, two, three = sums[i]
                product[first + i, pl.ds(row, 8), pl.ds(real, 128)] = one - two
                product[first + i, pl.ds(row, 8), pl.ds(imag, 128)] = three - one - two
        return carry

    lax.fori_loop(0, (share // 8) * lane_tiles, tile, 0)
    flat = product[...].astype(jnp.bfloat16).reshape(blocks * share, 2 * rows)
    for copy in copies[4:]:
        copy.wait()
    conv = jnp.dot(flat, inverse_ref[...], preferred_element_type=jnp.float32)
    mixer = signal_ref[:, :share, :].astype(jnp.float32)
    total = conv.reshape(blocks, share, rows) + gain_ref[...] * mixer
    sum_ref[...] = total.astype(jnp.bfloat16)
    quarters, width = out_ref.shape[1], out_ref.shape[3]
    for slot in range(quarters):
        start = (lax.axis_index("y") + STEPS[slot]) % quarters * width
        out_ref[:, slot] = sum_ref[:, :, pl.ds(pl.multiple_of(start, width), width)]


def gate(total, query, sides, out_ref, gated_ref):
    blocks, share, rows = total.shape
    half = blocks * share // 2
    for part, side in enumerate(sides):
        value = total[pl.ds(side * (blocks // 2), blocks // 2)].reshape(half, rows)
        channels = side * half if isinstance(side, int) else pl.multiple_of(side * half, half)
        value = query[:, pl.ds(channels, half)].astype(jnp.float32) * value.T.astype(jnp.float32)
        gated_ref[:, part * half : (part + 1) * half] = value.astype(jnp.bfloat16)
    piece = rows // 2
    keep = lax.axis_index("z")
    out_ref[:piece] = gated_ref[pl.ds(pl.multiple_of((1 - keep) * piece, piece), piece), :]
    out_ref[piece:] = gated_ref[pl.ds(pl.multiple_of(keep * piece, piece), piece), :]


def own_kernel(total_ref, query_ref, weight_ref, out_ref, blank_ref, gated_ref, rows_ref):
    del blank_ref
    rows = total_ref.shape[2]
    start = pl.multiple_of(lax.axis_index("y") * rows, rows)
    gate(total_ref, query_ref.at[pl.ds(start, rows)], (0, 1), rows_ref, gated_ref)
    for start in range(0, out_ref.shape[1], WIDTH):
        columns = slice(start, start + WIDTH)
        out_ref[:, columns] = jnp.dot(
            rows_ref[...], weight_ref[:, columns], preferred_element_type=jnp.float32
        )


def gate_kernel(*refs):
    totals, queries, out_ref, gated_ref = refs[:3], refs[3:6], refs[6], refs[7]
    core = lax.axis_index("core")
    depth = gated_ref.shape[1]
    for group in range(3):
        out = out_ref.at[:, pl.ds(group * depth, depth)]
        gate(totals[group], queries[group], (core, 1 - core), out, gated_ref)


def rest_kernel(first, gated_ref, partial_ref, *refs):
    weights, (other_ref, own_ref) = refs[:-2], refs[-2:]
    piece, columns = other_ref.shape
    for column in range(0, columns, WIDTH):
        here = slice(first + column, first + column + WIDTH)
        value, start = partial_ref[:, here], 0
        for weight in weights:
            depth = weight.shape[0]
            value = value + jnp.dot(
                gated_ref[:, start : start + depth],
                weight[:, here],
                preferred_element_type=jnp.float32,
            )
            start += depth
        value = value.astype(jnp.bfloat16)
        other_ref[:, column : column + WIDTH] = value[:piece]
        own_ref[:, column : column + WIDTH] = value[piece:]


VMEM = pl.BlockSpec(memory_space=pltpu.VMEM)
HBM = pl.BlockSpec(memory_space=pltpu.HBM)


def whole(kernel, shapes, in_specs, out_specs, scratch=(), limit=16, dtype=jnp.bfloat16, cost=0):
    return pl.pallas_call(
        kernel,
        out_shape=[
            jax.ShapeDtypeStruct(shape, dtype if i == 0 else jnp.bfloat16)
            for i, shape in enumerate(shapes)
        ],
        in_specs=in_specs,
        out_specs=out_specs,
        scratch_shapes=list(scratch),
        compiler_params=pltpu.CompilerParams(vmem_limit_bytes=limit * MIB),
        cost_estimate=pl.CostEstimate(flops=2 * cost, bytes_accessed=8 * MIB, transcendentals=0),
    )


def swap(axis):
    return lambda value: lax.ppermute(value, axis, [(0, 1), (1, 0)])


along_z, along_core = swap("z"), swap("core")


def along_y(value, steps):
    count = lax.axis_size("y")
    return lax.ppermute(value, "y", [(i, (i + steps) % count) for i in range(count)])


def add(*terms):
    return sum(term.astype(jnp.float32) for term in terms).astype(jnp.bfloat16)


def reduce_and_gather(halves):
    found, first, last = [], [], []
    arrived = [along_z(other) for other, _ in halves]
    for (_, own), from_z in zip(halves, arrived):
        own = add(own, from_z)
        first.append((own, along_z(own), along_y(own, 1), along_y(own, -1)))
    for stream, (own, own_z, down, up) in enumerate(first):
        own_z, down, up = lax.optimization_barrier((own_z, down, up))
        found += [(stream, 0, 0, own), (stream, 1, 0, own_z), (stream, 6, 0, down)]
        found.append((stream, 2, 0, up))
        last.append((along_z(up), along_y(up, -1), along_y(own_z, 1)))
    for stream, (up_z, far, down_z) in enumerate(last):
        up_z, far, down_z = lax.optimization_barrier((up_z, far, down_z))
        found += [(stream, 3, 0, up_z), (stream, 4, 0, far), (stream, 7, 0, down_z)]
        middle = up_z.shape[1] // 2
        found.append((stream, 5, 0, along_y(down_z[:, :middle], 1)))
        found.append((stream, 5, 1, along_y(up_z[:, middle:], -1)))
    return found


def body(query_branch, key_branch, value_branch, filters, skip_gain, out_weight):
    core, y, z = (lax.axis_index(name) for name in ("core", "y", "z"))
    ctx = lax.axis_index("block") * 2 + core
    ctx_count = lax.axis_size("block") * 2
    y_count = lax.axis_size("y")
    rows, channels = query_branch.shape
    share = channels // ctx_count
    features = out_weight.shape[1]
    quarter = rows // y_count
    forward, inverse = (jnp.asarray(table) for table in transform_tables(rows))
    gain = lax.dynamic_slice(skip_gain, (ctx * share,), (share,))[:, None]

    with jax.named_scope("pack"):
        square = pltpu.VMEM((rows, channels), jnp.bfloat16)
        outgoing, weight_half, to_up, to_down, to_far = whole(
            pack_kernel,
            [(ctx_count, 2 * share, rows), (channels // 2, features)] + [(quarter, channels)] * 3,
            [HBM] * 5,
            [VMEM] * 5,
            [square, square, square, pltpu.SemaphoreType.DMA((7,))],
            limit=60,
        )(key_branch, value_branch, filters, query_branch, out_weight)
    with jax.named_scope("weights"):
        weight_up, weight_down = along_y(weight_half, 1), along_y(weight_half, -1)
        query_up, query_down = along_y(to_up, 1), along_y(to_down, -1)
        query_far = along_y(to_far, 2)
    arrived = lax.all_to_all(outgoing, ("block", "core"), split_axis=0, concat_axis=0, tiled=True)
    spec = pltpu.VMEM((ctx_count, share, 2 * rows), jnp.float32)
    with jax.named_scope("conv"):
        (total,) = whole(
            conv_kernel,
            [(ctx_count, y_count, share, quarter)],
            [VMEM] * 2 + [HBM] * 2,
            [VMEM],
            [spec] * 3
            + [
                pltpu.VMEM(shape, jnp.bfloat16)
                for shape in ((ctx_count, share, rows), forward.shape, inverse.shape)
            ]
            + [pltpu.SemaphoreType.DMA((8,))],
            limit=24,
        )(arrived, gain, forward, inverse)
    with jax.named_scope("weights"):
        total, weight_up, weight_down, query_up, query_down, query_far = lax.optimization_barrier(
            (total, weight_up, weight_down, query_up, query_down, query_far)
        )
        cut = channels // 4
        far_first, far_last = along_y(weight_up[:cut], 1), along_y(weight_down[cut:], -1)
        swapped_up, swapped_down = along_core(weight_up), along_core(weight_down)
    total = lax.all_to_all(total, ("block", "core"), split_axis=0, concat_axis=0, tiled=True)
    with jax.named_scope("weights"):
        total, far_first, far_last, swapped_up, swapped_down = lax.optimization_barrier(
            (total, far_first, far_last, swapped_up, swapped_down)
        )
        swapped_first, swapped_last = along_core(far_first), along_core(far_last)
    with jax.named_scope("quarters"):
        total_up, total_down = along_y(total[:, 1], 1), along_y(total[:, 2], -1)
        total_far = along_y(total[:, 3], 2)
    with jax.named_scope("own"):
        gated = pltpu.VMEM((quarter, channels), jnp.bfloat16)
        partial_value, out = whole(
            own_kernel, [(quarter, features), (rows, features)], [VMEM] * 3, [VMEM, HBM],
            [gated, gated], limit=12, dtype=jnp.float32, cost=rows * channels * features,
        )(total[:, 0], query_branch, out_weight)
    with jax.named_scope("rest"):
        (rest,) = whole(gate_kernel, [(quarter, 3 * channels)], [VMEM] * 6, [VMEM], [gated])(
            total_up, total_down, total_far, query_up, query_down, query_far
        )
        weights = (
            weight_up, swapped_up, weight_down, swapped_down,
            far_first, far_last, swapped_first, swapped_last,
        )
        width = features // STREAMS
        halves = [
            whole(
                functools.partial(rest_kernel, stream * width),
                [(quarter // 2, width)] * 2,
                [VMEM] * (2 + len(weights)),
                [VMEM] * 2,
                limit=20,
                cost=rows * channels * features,
            )(rest, partial_value, *weights)
            for stream in range(STREAMS)
        ]
    slots = jnp.arange(2 * y_count, dtype=jnp.int32)
    order = ((y + slots // 2) % y_count * 2 + (z + slots) % 2) * (quarter // 2)
    with jax.named_scope("gather"):
        for stream, slot, part, value in reduce_and_gather(halves):
            column = stream * width + part * value.shape[1]
            out = lax.dynamic_update_slice(out, value, (order[slot], column))
    return out


def solution(mesh):
    fine = Mesh(mesh.devices.reshape(-1, 2, 4, 2), ("block", "core", "y", "z"))
    ctx, tp = ("block", "core"), ("y", "z")
    placed = (P(ctx, tp), P(ctx, tp), P(ctx, tp), P(ctx, tp), P(tp), P(tp, None))
    return jax.shard_map(
        body, mesh=fine, in_specs=placed, out_specs=P(ctx, None), check_vma=False
    )
```

```python
import functools
import math

import jax
import jax.numpy as jnp
import ml_dtypes
import numpy as np
from jax import lax
from jax.experimental import pallas as pl
from jax.experimental.pallas import tpu as pltpu
from jax.sharding import Mesh, PartitionSpec as P

MIB = 1024 * 1024
GROUP = 4
STREAMS = 2
WIDTH = 512


def transform_table(rows):
    j = np.arange(rows, dtype=np.int64)[:, None]
    f = np.arange(rows, dtype=np.int64)[None, :]
    angle = (j * (2 * f + 1) % (4 * rows)) * (2.0 * math.pi / (4 * rows))
    return np.concatenate([np.cos(angle), -np.sin(angle)], 1).astype(ml_dtypes.bfloat16)


def pack_kernel(
    key_hbm, value_hbm, filter_hbm, weight_hbm, out_ref, half_ref, key_ref, value_ref, filter_ref, sems
):
    parts, both, rows = out_ref.shape
    share, half = both // 2, half_ref.shape[0]
    start = pl.multiple_of(lax.axis_index("core") * half, half)
    moves = (
        (key_hbm, key_ref),
        (value_hbm, value_ref),
        (filter_hbm, filter_ref),
        (weight_hbm.at[pl.ds(start, half)], half_ref),
    )
    copies = [pltpu.make_async_copy(*move, sems.at[i]) for i, move in enumerate(moves)]
    for copy in copies:
        copy.start()
    copies[0].wait()
    copies[1].wait()
    mixer = key_ref[...].astype(jnp.float32) * value_ref[...].astype(jnp.float32)
    out_ref[:, :share, :] = mixer.astype(jnp.bfloat16).T.reshape(parts, share, rows)
    copies[2].wait()
    out_ref[:, share:, :] = filter_ref[...].T.reshape(parts, share, rows)
    copies[3].wait()


def conv_kernel(
    signal_ref, gain_ref, table_ref, out_ref, mixer_spec, filter_spec, product
):
    blocks, both, rows = signal_ref.shape
    share = both // 2
    table = table_ref[...]

    def spectrum(signal):
        flat = signal.reshape(blocks * share, rows)
        value = jnp.dot(flat, table, preferred_element_type=jnp.float32)
        return value.reshape(blocks, share, 2 * rows)

    mixer_spec[...] = spectrum(signal_ref[:, :share, :])
    filter_spec[...] = spectrum(signal_ref[:, share:, :])

    lane = lax.broadcasted_iota(jnp.int32, (8, 128), 1)
    sign = jnp.where(lane % 2 == 0, 1.0, -1.0).astype(jnp.float32)
    lane_tiles = rows // 128

    def tile(step, carry):
        row = pl.multiple_of((step // lane_tiles) * 8, 8)
        real = pl.multiple_of((step % lane_tiles) * 128, 128)
        imag = pl.multiple_of(rows + (step % lane_tiles) * 128, 128)

        def load(ref, block):
            return (
                ref[block, pl.ds(row, 8), pl.ds(real, 128)],
                ref[block, pl.ds(row, 8), pl.ds(imag, 128)],
            )

        def window(block):
            now_real, now_imag = load(mixer_spec, block)
            if block > 0:
                last_real, last_imag = load(mixer_spec, block - 1)
                now_real, now_imag = now_real - sign * last_imag, now_imag + sign * last_real
            return now_real, now_imag

        for block in reversed(range(blocks)):
            now_real, now_imag = window(block)
            mixer_spec[block, pl.ds(row, 8), pl.ds(real, 128)] = now_real
            mixer_spec[block, pl.ds(row, 8), pl.ds(imag, 128)] = now_imag

        for first in range(0, blocks, GROUP):
            sums = [[None] * 3 for _ in range(GROUP)]
            held = {}
            for lag in range(first + GROUP):
                filter_real, filter_imag = load(filter_spec, lag)
                filter_both = filter_real + filter_imag
                for i in range(GROUP):
                    block = first + i - lag
                    if block < 0:
                        continue
                    if block not in held:
                        real_part, imag_part = load(mixer_spec, block)
                        held[block] = (real_part, imag_part, real_part + imag_part)
                    terms = (
                        filter_real * held[block][0],
                        filter_imag * held[block][1],
                        filter_both * held[block][2],
                    )
                    for s in range(3):
                        sums[i][s] = terms[s] if sums[i][s] is None else sums[i][s] + terms[s]
                held.pop(first + GROUP - 1 - lag, None)
            for i in range(GROUP):
                one, two, three = sums[i]
                product[first + i, pl.ds(row, 8), pl.ds(real, 128)] = one - two
                product[first + i, pl.ds(row, 8), pl.ds(imag, 128)] = three - one - two
        return carry

    lax.fori_loop(0, (share // 8) * lane_tiles, tile, 0)
    flat = product[...].astype(jnp.bfloat16).reshape(blocks * share, 2 * rows)
    conv = lax.dot_general(
        flat, table, (((1,), (1,)), ((), ())), preferred_element_type=jnp.float32
    ) * (1.0 / rows)
    mixer = signal_ref[:, :share, :].astype(jnp.float32)
    total = conv.reshape(blocks, share, rows) + gain_ref[...] * mixer
    out_ref[...] = total.astype(jnp.bfloat16)


def gate_kernel(total_ref, query_ref, own_ref, toward_ref, back_ref, far_ref, gated_ref):
    rows, channels = query_ref.shape
    core, y, keep = lax.axis_index("core"), lax.axis_index("y"), lax.axis_index("z")
    total = total_ref[...].reshape(channels, rows).T.astype(jnp.float32)
    gated_ref[...] = (query_ref[...].astype(jnp.float32) * total).astype(jnp.bfloat16)
    half, piece = channels // 2, own_ref.shape[0] // 2
    steps = (own_ref, y), (toward_ref, y + 1 - 2 * core), (back_ref, y + 3 + 2 * core)
    for out_ref, place in steps + ((far_ref, y + 2),):
        for part, side in enumerate((1 - keep, keep)):
            start = pl.multiple_of((place % 4 * 2 + side) * piece, piece)
            rows_out = slice(part * piece, (part + 1) * piece)
            if out_ref is own_ref:
                out_ref[rows_out, :] = gated_ref[pl.ds(start, piece), :]
                continue
            for column, sender in enumerate((core, 1 - core)):
                columns = pl.ds(pl.multiple_of(sender * half, half), half)
                here = slice(column * half, (column + 1) * half)
                out_ref[rows_out, here] = gated_ref[pl.ds(start, piece), columns]


def own_kernel(gated_ref, weight_ref, out_ref):
    for start in range(0, out_ref.shape[1], WIDTH):
        columns = slice(start, start + WIDTH)
        out_ref[:, columns] = jnp.dot(
            gated_ref[...], weight_ref[:, columns], preferred_element_type=jnp.float32
        )


def rest_kernel(first, partial_ref, *refs):
    gated, weights, (other_ref, own_ref) = refs[:3], refs[3:-2], refs[-2:]
    piece, columns = other_ref.shape
    depth = weights[0].shape[0]
    for column in range(0, columns, WIDTH):
        here = slice(first + column, first + column + WIDTH)
        value = partial_ref[:, here]
        for i, weight in enumerate(weights):
            half = slice(i % 2 * depth, (i % 2 + 1) * depth)
            value = value + jnp.dot(
                gated[i // 2][:, half], weight[:, here], preferred_element_type=jnp.float32
            )
        value = value.astype(jnp.bfloat16)
        other_ref[:, column : column + WIDTH] = value[:piece]
        own_ref[:, column : column + WIDTH] = value[piece:]


def place_kernel(layout, fresh, *refs):
    pieces, (out_ref, sems) = refs[0 if fresh else 1 : -2], refs[-2:]
    y, z = lax.axis_index("y"), lax.axis_index("z")
    copies = []
    for i, (piece, (slot, column)) in enumerate(zip(pieces, layout)):
        count, width = piece.shape
        row = ((y + slot // 2) % 4 * 2 + (z + slot) % 2) * count
        target = out_ref.at[pl.ds(pl.multiple_of(row, count), count), pl.ds(column, width)]
        copies.append(pltpu.make_async_copy(piece, target, sems.at[i]))
    for copy in copies:
        copy.start()
    for copy in copies:
        copy.wait()


VMEM = pl.BlockSpec(memory_space=pltpu.VMEM)
HBM = pl.BlockSpec(memory_space=pltpu.HBM)


def whole(kernel, shapes, in_specs, out_specs, scratch=(), limit=16, cost=0, **rest):
    return pl.pallas_call(
        kernel,
        out_shape=[jax.ShapeDtypeStruct(*shape) for shape in shapes],
        in_specs=in_specs,
        out_specs=out_specs,
        scratch_shapes=list(scratch),
        compiler_params=pltpu.CompilerParams(vmem_limit_bytes=limit * MIB),
        cost_estimate=pl.CostEstimate(flops=2 * cost, bytes_accessed=8 * MIB, transcendentals=0),
        **rest,
    )


def place_pieces(out, shape, found):
    fresh = out is None
    layout, values = [item[:2] for item in found], [item[2] for item in found]
    return whole(
        functools.partial(place_kernel, layout, fresh),
        [(shape, jnp.bfloat16)],
        [HBM] * (not fresh) + [VMEM] * len(values),
        [HBM],
        [pltpu.SemaphoreType.DMA((len(values),))],
        input_output_aliases={} if fresh else {0: 0},
    )(*([] if fresh else [out]), *values)[0]


def swap(axis):
    return lambda value: lax.ppermute(value, axis, [(0, 1), (1, 0)])


along_z, along_core = swap("z"), swap("core")


def along_y(value, steps):
    count = lax.axis_size("y")
    return lax.ppermute(value, "y", [(i, (i + steps) % count) for i in range(count)])


def mirrored(value, steps):
    count = lax.axis_size("y")
    pairs = [
        (core * count + i, core * count + (i + (steps, -steps)[core]) % count)
        for core in range(2)
        for i in range(count)
    ]
    return lax.ppermute(value, ("core", "y"), pairs)


def add(*terms):
    return sum(term.astype(jnp.float32) for term in terms).astype(jnp.bfloat16)


def reduce_and_gather(halves, shape):
    first, last, early, late = [], [], [], []
    width = halves[0][1].shape[1]
    arrived = [along_z(other) for other, _ in halves]
    for (_, own), from_z in zip(halves, arrived):
        own = add(own, from_z)
        first.append((own, along_z(own), along_y(own, 1), along_y(own, -1)))
    for stream, (own, own_z, down, up) in enumerate(first):
        column = stream * width
        own_z, down, up = lax.optimization_barrier((own_z, down, up))
        early += [(slot, column, value) for slot, value in ((0, own), (1, own_z), (6, down), (2, up))]
        last.append((along_z(up), along_y(up, -1), along_y(own_z, 1)))
    out = place_pieces(None, shape, early)
    for stream, (up_z, far, down_z) in enumerate(last):
        column = stream * width
        up_z, far, down_z = lax.optimization_barrier((up_z, far, down_z))
        late += [(3, column, up_z), (4, column, far), (7, column, down_z)]
        middle = width // 2
        late.append((5, column, along_y(down_z[:, :middle], 1)))
        late.append((5, column + middle, along_y(up_z[:, middle:], -1)))
    return place_pieces(out, shape, late)


def body(query_branch, key_branch, value_branch, filters, skip_gain, out_weight):
    ctx = lax.axis_index("block") * 2 + lax.axis_index("core")
    ctx_count = lax.axis_size("block") * 2
    rows, channels = query_branch.shape
    share = channels // ctx_count
    features = out_weight.shape[1]
    quarter = rows // lax.axis_size("y")
    half16, full32 = jnp.bfloat16, jnp.float32
    table = jnp.asarray(transform_table(rows))
    gain = lax.dynamic_slice(skip_gain, (ctx * share,), (share,))[:, None]

    with jax.named_scope("pack"):
        square = pltpu.VMEM((rows, channels), half16)
        outgoing, weight_half = whole(
            pack_kernel,
            [((ctx_count, 2 * share, rows), half16), ((channels // 2, features), half16)],
            [HBM] * 4,
            [VMEM] * 2,
            [square, square, square, pltpu.SemaphoreType.DMA((4,))],
            limit=60,
        )(key_branch, value_branch, filters, out_weight)
    with jax.named_scope("weights"):
        toward, back = mirrored(weight_half, 1), mirrored(weight_half, -1)
    arrived = lax.all_to_all(outgoing, ("block", "core"), split_axis=0, concat_axis=0, tiled=True)
    spec = pltpu.VMEM((ctx_count, share, 2 * rows), full32)
    with jax.named_scope("conv"):
        (total,) = whole(
            conv_kernel,
            [((ctx_count, share, rows), half16)],
            [VMEM] * 3,
            [VMEM],
            [spec] * 3,
            limit=24,
        )(arrived, gain, table)
    with jax.named_scope("weights"):
        total, toward, back = lax.optimization_barrier((total, toward, back))
        far = mirrored(toward, 1)
        swapped = [along_core(toward), along_core(back)]
    total = lax.all_to_all(total, ("block", "core"), split_axis=0, concat_axis=0, tiled=True)
    with jax.named_scope("weights"):
        total, far, *swapped = lax.optimization_barrier((total, far, *swapped))
        weights = (toward, swapped[1], back, swapped[0], far, along_core(far))
    with jax.named_scope("gate"):
        gated = whole(
            gate_kernel, [((quarter, channels), half16)] * 4, [VMEM] * 2, [VMEM] * 4, [square]
        )(total, query_branch)
    with jax.named_scope("quarters"):
        others = mirrored(gated[1], 1), mirrored(gated[2], -1), along_y(gated[3], 2)
    cost = quarter * channels * features
    with jax.named_scope("own"):
        (partial_value,) = whole(
            own_kernel, [((quarter, features), full32)], [VMEM] * 2, [VMEM], limit=12, cost=cost
        )(gated[0], out_weight)
    with jax.named_scope("rest"):
        width = features // STREAMS
        halves = [
            whole(
                functools.partial(rest_kernel, stream * width),
                [((quarter // 2, width), half16)] * 2,
                [VMEM] * (4 + len(weights)),
                [VMEM] * 2,
                limit=20,
                cost=cost,
            )(partial_value, *others, *weights)
            for stream in range(STREAMS)
        ]
    with jax.named_scope("gather"):
        return reduce_and_gather(halves, (rows, features))


def solution(mesh):
    fine = Mesh(mesh.devices.reshape(-1, 2, 4, 2), ("block", "core", "y", "z"))
    ctx, tp = ("block", "core"), ("y", "z")
    placed = (P(ctx, tp), P(ctx, tp), P(ctx, tp), P(ctx, tp), P(tp), P(tp, None))
    return jax.shard_map(
        body, mesh=fine, in_specs=placed, out_specs=P(ctx, None), check_vma=False
    )
```

```python
import functools
import math

import jax
import jax.numpy as jnp
import ml_dtypes
import numpy as np
from jax import lax
from jax.experimental import pallas as pl
from jax.experimental.pallas import tpu as pltpu
from jax.sharding import Mesh, PartitionSpec as P

MIB = 1024 * 1024
GROUP = 4
PIECES = 4
STREAMS = 2
WIDTH = 512


def transform_table(rows):
    j = np.arange(rows, dtype=np.int64)[:, None]
    f = np.arange(rows, dtype=np.int64)[None, :]
    angle = (j * (2 * f + 1) % (4 * rows)) * (2.0 * math.pi / (4 * rows))
    return np.concatenate([np.cos(angle), -np.sin(angle)], 1).astype(ml_dtypes.bfloat16)


def pack_kernel(
    key_hbm, value_hbm, filter_hbm, weight_hbm, out_hbm, half_hbm,
    key_ref, value_ref, filter_ref, half_ref, out_ref, sems,
):
    parts, both, rows = out_hbm.shape
    share, half = both // 2, half_hbm.shape[0]
    start = pl.multiple_of(lax.axis_index("core") * half, half)
    piece = half // PIECES
    moves = [(key_hbm, key_ref), (value_hbm, value_ref), (filter_hbm, filter_ref)]
    for i in range(PIECES):
        here = pl.ds(i * piece, piece)
        moves.append((weight_hbm.at[pl.ds(start + i * piece, piece)], half_ref.at[here]))
    arriving = [pltpu.make_async_copy(*move, sems.at[i]) for i, move in enumerate(moves)]
    leaving = []

    def send(source, target):
        leaving.append(pltpu.make_async_copy(source, target, sems.at[len(moves) + len(leaving)]))
        leaving[-1].start()

    for copy in arriving:
        copy.start()
    arriving[0].wait()
    arriving[1].wait()
    mixer = key_ref[...].astype(jnp.float32) * value_ref[...].astype(jnp.float32)
    out_ref[:, :share, :] = mixer.astype(jnp.bfloat16).T.reshape(parts, share, rows)
    send(out_ref.at[:, pl.ds(0, share)], out_hbm.at[:, pl.ds(0, share)])
    arriving[2].wait()
    out_ref[:, share:, :] = filter_ref[...].T.reshape(parts, share, rows)
    send(out_ref.at[:, pl.ds(share, share)], out_hbm.at[:, pl.ds(share, share)])
    for i in range(PIECES):
        arriving[3 + i].wait()
        here = pl.ds(i * piece, piece)
        send(half_ref.at[here], half_hbm.at[here])
    for copy in leaving:
        copy.wait()


def conv_kernel(signal_ref, gain_ref, table_ref, out_ref, mixer_spec, filter_spec, product):
    blocks, both, rows = signal_ref.shape
    share = both // 2
    table = table_ref[...]
    lane = lax.broadcasted_iota(jnp.int32, (8, 128), 1)
    sign = jnp.where(lane % 2 == 0, 1.0, -1.0).astype(jnp.float32)
    for part, spec in enumerate((mixer_spec, filter_spec)):
        flat = signal_ref[:, part * share : (part + 1) * share, :].reshape(blocks * share, rows)
        value = jnp.dot(flat, table, preferred_element_type=jnp.float32)
        spec[...] = value.reshape(blocks, share, 2 * rows)

    for column in range(0, rows, 128):
        real, imag = slice(column, column + 128), slice(rows + column, rows + column + 128)
        for row in range(0, share, 8):
            here = slice(row, row + 8)

            def load(ref, block):
                return ref[block, here, real], ref[block, here, imag]

            for block in reversed(range(1, blocks)):
                now_real, now_imag = load(mixer_spec, block)
                last_real, last_imag = load(mixer_spec, block - 1)
                mixer_spec[block, here, real] = now_real - sign * last_imag
                mixer_spec[block, here, imag] = now_imag + sign * last_real

            for first in range(0, blocks, GROUP):
                sums = [[None] * 3 for _ in range(GROUP)]
                held = {}
                for lag in range(first + GROUP):
                    filter_real, filter_imag = load(filter_spec, lag)
                    filter_both = filter_real + filter_imag
                    for i in range(GROUP):
                        block = first + i - lag
                        if block < 0:
                            continue
                        if block not in held:
                            real_part, imag_part = load(mixer_spec, block)
                            held[block] = (real_part, imag_part, real_part + imag_part)
                        terms = (
                            filter_real * held[block][0],
                            filter_imag * held[block][1],
                            filter_both * held[block][2],
                        )
                        for s in range(3):
                            sums[i][s] = terms[s] if sums[i][s] is None else sums[i][s] + terms[s]
                    held.pop(first + GROUP - 1 - lag, None)
                for i in range(GROUP):
                    one, two, three = sums[i]
                    product[first + i, here, real] = one - two
                    product[first + i, here, imag] = three - one - two

    flat = product[...].astype(jnp.bfloat16).reshape(blocks * share, 2 * rows)
    conv = lax.dot_general(
        flat, table, (((1,), (1,)), ((), ())), preferred_element_type=jnp.float32
    ) * (1.0 / rows)
    mixer = signal_ref[:, :share, :].astype(jnp.float32)
    total = conv.reshape(blocks, share, rows) + gain_ref[...] * mixer
    out_ref[...] = total.astype(jnp.bfloat16)


def gate_kernel(total_ref, query_ref, own_ref, toward_ref, back_ref, far_ref, gated_ref):
    rows, channels = query_ref.shape
    core, y, keep = lax.axis_index("core"), lax.axis_index("y"), lax.axis_index("z")
    total = total_ref[...].reshape(channels, rows).T.astype(jnp.float32)
    gated_ref[...] = (query_ref[...].astype(jnp.float32) * total).astype(jnp.bfloat16)
    half, piece = channels // 2, own_ref.shape[0] // 2
    steps = (own_ref, y), (toward_ref, y + 1 - 2 * core), (back_ref, y + 3 + 2 * core)
    for out_ref, place in steps + ((far_ref, y + 2),):
        for part, side in enumerate((1 - keep, keep)):
            start = pl.multiple_of((place % 4 * 2 + side) * piece, piece)
            rows_out = slice(part * piece, (part + 1) * piece)
            if out_ref is own_ref:
                out_ref[rows_out, :] = gated_ref[pl.ds(start, piece), :]
                continue
            for column, sender in enumerate((core, 1 - core)):
                columns = pl.ds(pl.multiple_of(sender * half, half), half)
                here = slice(column * half, (column + 1) * half)
                out_ref[rows_out, here] = gated_ref[pl.ds(start, piece), columns]


def own_kernel(gated_ref, weight_ref, out_ref):
    for start in range(0, out_ref.shape[1], WIDTH):
        columns = slice(start, start + WIDTH)
        out_ref[:, columns] = jnp.dot(
            gated_ref[...], weight_ref[:, columns], preferred_element_type=jnp.float32
        )


def rest_kernel(first, partial_ref, *refs):
    gated, weights, (other_ref, own_ref) = refs[:3], refs[3:-2], refs[-2:]
    piece, columns = other_ref.shape
    depth = weights[0].shape[0]
    for column in range(0, columns, WIDTH):
        here = slice(first + column, first + column + WIDTH)
        value = partial_ref[:, here]
        for i, weight in enumerate(weights):
            half = slice(i % 2 * depth, (i % 2 + 1) * depth)
            value = value + jnp.dot(
                gated[i // 2][:, half], weight[:, here], preferred_element_type=jnp.float32
            )
        value = value.astype(jnp.bfloat16)
        other_ref[:, column : column + WIDTH] = value[:piece]
        own_ref[:, column : column + WIDTH] = value[piece:]


def place_kernel(layout, fresh, *refs):
    pieces, (out_ref, sems) = refs[0 if fresh else 1 : -2], refs[-2:]
    y, z = lax.axis_index("y"), lax.axis_index("z")
    copies = []
    for i, (piece, (slot, column)) in enumerate(zip(pieces, layout)):
        count, width = piece.shape
        row = ((y + slot // 2) % 4 * 2 + (z + slot) % 2) * count
        target = out_ref.at[pl.ds(pl.multiple_of(row, count), count), pl.ds(column, width)]
        copies.append(pltpu.make_async_copy(piece, target, sems.at[i]))
    for copy in copies:
        copy.start()
    for copy in copies:
        copy.wait()


VMEM = pl.BlockSpec(memory_space=pltpu.VMEM)
HBM = pl.BlockSpec(memory_space=pltpu.HBM)


def whole(kernel, shapes, in_specs, out_specs, scratch=(), limit=16, cost=0, **rest):
    return pl.pallas_call(
        kernel,
        out_shape=[jax.ShapeDtypeStruct(*shape) for shape in shapes],
        in_specs=in_specs,
        out_specs=out_specs,
        scratch_shapes=list(scratch),
        compiler_params=pltpu.CompilerParams(vmem_limit_bytes=limit * MIB),
        cost_estimate=pl.CostEstimate(flops=2 * cost, bytes_accessed=8 * MIB, transcendentals=0),
        **rest,
    )


def place_pieces(out, shape, found):
    fresh = out is None
    layout, values = [item[:2] for item in found], [item[2] for item in found]
    return whole(
        functools.partial(place_kernel, layout, fresh),
        [(shape, jnp.bfloat16)],
        [HBM] * (not fresh) + [VMEM] * len(values),
        [HBM],
        [pltpu.SemaphoreType.DMA((len(values),))],
        input_output_aliases={} if fresh else {0: 0},
    )(*([] if fresh else [out]), *values)[0]


def swap(axis):
    return lambda value: lax.ppermute(value, axis, [(0, 1), (1, 0)])


along_z, along_core = swap("z"), swap("core")


def along_y(value, steps):
    count = lax.axis_size("y")
    return lax.ppermute(value, "y", [(i, (i + steps) % count) for i in range(count)])


def mirrored(value, steps):
    count = lax.axis_size("y")
    pairs = [
        (core * count + i, core * count + (i + (steps, -steps)[core]) % count)
        for core in range(2)
        for i in range(count)
    ]
    return lax.ppermute(value, ("core", "y"), pairs)


def add(*terms):
    return sum(term.astype(jnp.float32) for term in terms).astype(jnp.bfloat16)


def reduce_and_gather(halves, shape):
    first, last, early, late = [], [], [], []
    width = halves[0][1].shape[1]
    arrived = [along_z(other) for other, _ in halves]
    for (_, own), from_z in zip(halves, arrived):
        own = add(own, from_z)
        first.append((own, along_z(own), along_y(own, 1), along_y(own, -1)))
    for stream, (own, own_z, down, up) in enumerate(first):
        column = stream * width
        own_z, down, up = lax.optimization_barrier((own_z, down, up))
        early += [(slot, column, value) for slot, value in ((0, own), (1, own_z), (6, down), (2, up))]
        last.append((along_z(up), along_y(up, -1), along_y(own_z, 1)))
    out = place_pieces(None, shape, early)
    for stream, (up_z, far, down_z) in enumerate(last):
        column = stream * width
        up_z, far, down_z = lax.optimization_barrier((up_z, far, down_z))
        late += [(3, column, up_z), (4, column, far), (7, column, down_z)]
        middle = width // 2
        late.append((5, column, along_y(down_z[:, :middle], 1)))
        late.append((5, column + middle, along_y(up_z[:, middle:], -1)))
    return place_pieces(out, shape, late)


def body(query_branch, key_branch, value_branch, filters, skip_gain, out_weight):
    ctx = lax.axis_index("block") * 2 + lax.axis_index("core")
    ctx_count = lax.axis_size("block") * 2
    rows, channels = query_branch.shape
    share = channels // ctx_count
    features = out_weight.shape[1]
    quarter = rows // lax.axis_size("y")
    half16, full32 = jnp.bfloat16, jnp.float32
    table = jnp.asarray(transform_table(rows))
    gain = lax.dynamic_slice(skip_gain, (ctx * share,), (share,))[:, None]

    with jax.named_scope("pack"):
        square = pltpu.VMEM((rows, channels), half16)
        outgoing, weight_half = whole(
            pack_kernel,
            [((ctx_count, 2 * share, rows), half16), ((channels // 2, features), half16)],
            [HBM] * 4,
            [HBM] * 2,
            [
                square,
                square,
                square,
                pltpu.VMEM((channels // 2, features), half16),
                pltpu.VMEM((ctx_count, 2 * share, rows), half16),
                pltpu.SemaphoreType.DMA((5 + 2 * PIECES,)),
            ],
            limit=60,
        )(key_branch, value_branch, filters, out_weight)
    with jax.named_scope("weights"):
        toward, back = mirrored(weight_half, 1), mirrored(weight_half, -1)
    arrived = lax.all_to_all(outgoing, ("block", "core"), split_axis=0, concat_axis=0, tiled=True)
    spec = pltpu.VMEM((ctx_count, share, 2 * rows), full32)
    with jax.named_scope("conv"):
        (total,) = whole(
            conv_kernel,
            [((ctx_count, share, rows), half16)],
            [VMEM] * 3,
            [VMEM],
            [spec] * 3,
            limit=24,
        )(arrived, gain, table)
    with jax.named_scope("weights"):
        total, toward, back = lax.optimization_barrier((total, toward, back))
        far = mirrored(toward, 1)
        swapped = [along_core(toward), along_core(back)]
    total = lax.all_to_all(total, ("block", "core"), split_axis=0, concat_axis=0, tiled=True)
    with jax.named_scope("weights"):
        total, far, *swapped = lax.optimization_barrier((total, far, *swapped))
        weights = (toward, swapped[1], back, swapped[0], far, along_core(far))
    with jax.named_scope("gate"):
        gated = whole(
            gate_kernel, [((quarter, channels), half16)] * 4, [VMEM] * 2, [VMEM] * 4, [square]
        )(total, query_branch)
    with jax.named_scope("quarters"):
        others = mirrored(gated[1], 1), mirrored(gated[2], -1), along_y(gated[3], 2)
    cost = quarter * channels * features
    with jax.named_scope("own"):
        (partial_value,) = whole(
            own_kernel, [((quarter, features), full32)], [VMEM] * 2, [VMEM], limit=12, cost=cost
        )(gated[0], out_weight)
    with jax.named_scope("rest"):
        width = features // STREAMS
        halves = [
            whole(
                functools.partial(rest_kernel, stream * width),
                [((quarter // 2, width), half16)] * 2,
                [VMEM] * (4 + len(weights)),
                [VMEM] * 2,
                limit=20,
                cost=cost,
            )(partial_value, *others, *weights)
            for stream in range(STREAMS)
        ]
    with jax.named_scope("gather"):
        return reduce_and_gather(halves, (rows, features))


def solution(mesh):
    fine = Mesh(mesh.devices.reshape(-1, 2, 4, 2), ("block", "core", "y", "z"))
    ctx, tp = ("block", "core"), ("y", "z")
    placed = (P(ctx, tp), P(ctx, tp), P(ctx, tp), P(ctx, tp), P(tp), P(tp, None))
    return jax.shard_map(
        body, mesh=fine, in_specs=placed, out_specs=P(ctx, None), check_vma=False
    )
```

```python
import functools
import math

import jax
import jax.numpy as jnp
import ml_dtypes
import numpy as np
from jax import lax
from jax.experimental import pallas as pl
from jax.experimental.pallas import tpu as pltpu
from jax.sharding import Mesh, PartitionSpec as P

MIB = 1024 * 1024
GROUP = 4
PIECES = 4
STREAMS = 2
WIDTH = 512


def transform_table(rows):
    j = np.arange(rows, dtype=np.int64)[:, None]
    f = np.arange(rows, dtype=np.int64)[None, :]
    angle = (j * (2 * f + 1) % (4 * rows)) * (2.0 * math.pi / (4 * rows))
    return np.concatenate([np.cos(angle), -np.sin(angle)], 1).astype(ml_dtypes.bfloat16)


def pack_kernel(
    key_hbm, value_hbm, filter_hbm, weight_hbm, out_hbm, half_hbm,
    key_ref, value_ref, filter_ref, half_ref, out_ref, sems,
):
    parts, both, rows = out_hbm.shape
    share, half = both // 2, half_hbm.shape[0]
    start = pl.multiple_of(lax.axis_index("core") * half, half)
    piece = half // PIECES
    moves = [(key_hbm, key_ref), (value_hbm, value_ref), (filter_hbm, filter_ref)]
    for i in range(PIECES):
        here = pl.ds(i * piece, piece)
        moves.append((weight_hbm.at[pl.ds(start + i * piece, piece)], half_ref.at[here]))
    arriving = [pltpu.make_async_copy(*move, sems.at[i]) for i, move in enumerate(moves)]
    leaving = []

    def send(source, target):
        leaving.append(pltpu.make_async_copy(source, target, sems.at[len(moves) + len(leaving)]))
        leaving[-1].start()

    for copy in arriving:
        copy.start()
    arriving[0].wait()
    arriving[1].wait()
    mixer = key_ref[...].astype(jnp.float32) * value_ref[...].astype(jnp.float32)
    out_ref[:, :share, :] = mixer.astype(jnp.bfloat16).T.reshape(parts, share, rows)
    send(out_ref.at[:, pl.ds(0, share)], out_hbm.at[:, pl.ds(0, share)])
    arriving[2].wait()
    out_ref[:, share:, :] = filter_ref[...].T.reshape(parts, share, rows)
    send(out_ref.at[:, pl.ds(share, share)], out_hbm.at[:, pl.ds(share, share)])
    for i in range(PIECES):
        arriving[3 + i].wait()
        here = pl.ds(i * piece, piece)
        send(half_ref.at[here], half_hbm.at[here])
    for copy in leaving:
        copy.wait()


def conv_kernel(signal_ref, gain_ref, table_ref, out_ref, mixer_spec, filter_spec, product):
    blocks, both, rows = signal_ref.shape
    share = both // 2
    table = table_ref[...]
    lane = lax.broadcasted_iota(jnp.int32, (8, 128), 1)
    sign = jnp.where(lane % 2 == 0, 1.0, -1.0).astype(jnp.float32)
    for part, spec in enumerate((mixer_spec, filter_spec)):
        flat = signal_ref[:, part * share : (part + 1) * share, :].reshape(blocks * share, rows)
        value = jnp.dot(flat, table, preferred_element_type=jnp.float32)
        spec[...] = value.reshape(blocks, share, 2 * rows)

    for column in range(0, rows, 128):
        real, imag = slice(column, column + 128), slice(rows + column, rows + column + 128)
        for row in range(0, share, 8):
            here = slice(row, row + 8)

            def load(ref, block):
                return ref[block, here, real], ref[block, here, imag]

            for block in reversed(range(1, blocks)):
                now_real, now_imag = load(mixer_spec, block)
                last_real, last_imag = load(mixer_spec, block - 1)
                mixer_spec[block, here, real] = now_real - sign * last_imag
                mixer_spec[block, here, imag] = now_imag + sign * last_real

            for first in range(0, blocks, GROUP):
                sums = [[None] * 3 for _ in range(GROUP)]
                held = {}
                for lag in range(first + GROUP):
                    filter_real, filter_imag = load(filter_spec, lag)
                    filter_both = filter_real + filter_imag
                    for i in range(GROUP):
                        block = first + i - lag
                        if block < 0:
                            continue
                        if block not in held:
                            real_part, imag_part = load(mixer_spec, block)
                            held[block] = (real_part, imag_part, real_part + imag_part)
                        terms = (
                            filter_real * held[block][0],
                            filter_imag * held[block][1],
                            filter_both * held[block][2],
                        )
                        for s in range(3):
                            sums[i][s] = terms[s] if sums[i][s] is None else sums[i][s] + terms[s]
                    held.pop(first + GROUP - 1 - lag, None)
                for i in range(GROUP):
                    one, two, three = sums[i]
                    product[first + i, here, real] = one - two
                    product[first + i, here, imag] = three - one - two

    flat = product[...].astype(jnp.bfloat16).reshape(blocks * share, 2 * rows)
    conv = lax.dot_general(
        flat, table, (((1,), (1,)), ((), ())), preferred_element_type=jnp.float32
    ) * (1.0 / rows)
    mixer = signal_ref[:, :share, :].astype(jnp.float32)
    total = conv.reshape(blocks, share, rows) + gain_ref[...] * mixer
    out_ref[...] = total.astype(jnp.bfloat16)


def gate_kernel(total_ref, query_ref, own_ref, toward_ref, back_ref, far_ref, gated_ref):
    rows, channels = query_ref.shape
    core, y, keep = lax.axis_index("core"), lax.axis_index("y"), lax.axis_index("z")
    total = total_ref[...].reshape(channels, rows).T.astype(jnp.float32)
    gated_ref[...] = (query_ref[...].astype(jnp.float32) * total).astype(jnp.bfloat16)
    half, piece = channels // 2, own_ref.shape[0] // 2
    steps = (own_ref, y), (toward_ref, y + 1 - 2 * core), (back_ref, y + 3 + 2 * core)
    for out_ref, place in steps + ((far_ref, y + 2),):
        for part, side in enumerate((1 - keep, keep)):
            start = pl.multiple_of((place % 4 * 2 + side) * piece, piece)
            rows_out = slice(part * piece, (part + 1) * piece)
            if out_ref is own_ref:
                out_ref[rows_out, :] = gated_ref[pl.ds(start, piece), :]
                continue
            for column, sender in enumerate((core, 1 - core)):
                columns = pl.ds(pl.multiple_of(sender * half, half), half)
                here = slice(column * half, (column + 1) * half)
                out_ref[rows_out, here] = gated_ref[pl.ds(start, piece), columns]


def own_kernel(gated_ref, weight_ref, out_ref):
    for start in range(0, out_ref.shape[1], WIDTH):
        columns = slice(start, start + WIDTH)
        out_ref[:, columns] = jnp.dot(
            gated_ref[...], weight_ref[:, columns], preferred_element_type=jnp.float32
        )


def rest_kernel(first, partial_ref, *refs):
    gated, weights, (other_ref, own_ref) = refs[:3], refs[3:-2], refs[-2:]
    piece, columns = other_ref.shape
    depth = weights[0].shape[0]
    for column in range(0, columns, WIDTH):
        here = slice(first + column, first + column + WIDTH)
        value = partial_ref[:, here]
        for i, weight in enumerate(weights):
            half = slice(i % 2 * depth, (i % 2 + 1) * depth)
            value = value + jnp.dot(
                gated[i // 2][:, half], weight[:, here], preferred_element_type=jnp.float32
            )
        value = value.astype(jnp.bfloat16)
        other_ref[:, column : column + WIDTH] = value[:piece]
        own_ref[:, column : column + WIDTH] = value[piece:]


def place_kernel(layout, fresh, *refs):
    pieces, (out_ref, sems) = refs[0 if fresh else 1 : -2], refs[-2:]
    y, z = lax.axis_index("y"), lax.axis_index("z")
    copies = []
    for i, (piece, (slot, column)) in enumerate(zip(pieces, layout)):
        count, width = piece.shape
        row = ((y + slot // 2) % 4 * 2 + (z + slot) % 2) * count
        target = out_ref.at[pl.ds(pl.multiple_of(row, count), count), pl.ds(column, width)]
        copies.append(pltpu.make_async_copy(piece, target, sems.at[i]))
    for copy in copies:
        copy.start()
    for copy in copies:
        copy.wait()


VMEM = pl.BlockSpec(memory_space=pltpu.VMEM)
HBM = pl.BlockSpec(memory_space=pltpu.HBM)


def whole(kernel, shapes, in_specs, out_specs, scratch=(), limit=16, cost=0, **rest):
    return pl.pallas_call(
        kernel,
        out_shape=[jax.ShapeDtypeStruct(*shape) for shape in shapes],
        in_specs=in_specs,
        out_specs=out_specs,
        scratch_shapes=list(scratch),
        compiler_params=pltpu.CompilerParams(vmem_limit_bytes=limit * MIB),
        cost_estimate=pl.CostEstimate(flops=2 * cost, bytes_accessed=8 * MIB, transcendentals=0),
        **rest,
    )


def place_pieces(out, shape, found):
    fresh = out is None
    layout, values = [item[:2] for item in found], [item[2] for item in found]
    return whole(
        functools.partial(place_kernel, layout, fresh),
        [(shape, jnp.bfloat16)],
        [HBM] * (not fresh) + [VMEM] * len(values),
        [HBM],
        [pltpu.SemaphoreType.DMA((len(values),))],
        input_output_aliases={} if fresh else {0: 0},
    )(*([] if fresh else [out]), *values)[0]


def swap(axis):
    return lambda value: lax.ppermute(value, axis, [(0, 1), (1, 0)])


along_z, along_core = swap("z"), swap("core")


def along_y(value, steps):
    count = lax.axis_size("y")
    return lax.ppermute(value, "y", [(i, (i + steps) % count) for i in range(count)])


def mirrored(value, steps):
    count = lax.axis_size("y")
    pairs = [
        (core * count + i, core * count + (i + (steps, -steps)[core]) % count)
        for core in range(2)
        for i in range(count)
    ]
    return lax.ppermute(value, ("core", "y"), pairs)


def add(*terms):
    return sum(term.astype(jnp.float32) for term in terms).astype(jnp.bfloat16)


def reduce_and_gather(halves, shape):
    first, last, early, late = [], [], [], []
    width = halves[0][1].shape[1]
    arrived = [along_z(other) for other, _ in halves]
    for (_, own), from_z in zip(halves, arrived):
        own = add(own, from_z)
        first.append((own, along_z(own), along_y(own, 1), along_y(own, -1)))
    for stream, (own, own_z, down, up) in enumerate(first):
        column = stream * width
        own_z, down, up = lax.optimization_barrier((own_z, down, up))
        early += [(slot, column, value) for slot, value in ((0, own), (1, own_z), (6, down), (2, up))]
        last.append((along_z(up), along_y(up, -1), along_y(own_z, 1)))
    out = place_pieces(None, shape, early)
    for stream, (up_z, far, down_z) in enumerate(last):
        column = stream * width
        up_z, far, down_z = lax.optimization_barrier((up_z, far, down_z))
        late += [(3, column, up_z), (4, column, far), (7, column, down_z)]
        middle = width // 2
        late.append((5, column, along_y(down_z[:, :middle], 1)))
        late.append((5, column + middle, along_y(up_z[:, middle:], -1)))
    return place_pieces(out, shape, late)


def body(query_branch, key_branch, value_branch, filters, skip_gain, out_weight):
    ctx = lax.axis_index("block") * 2 + lax.axis_index("core")
    ctx_count = lax.axis_size("block") * 2
    rows, channels = query_branch.shape
    share = channels // ctx_count
    features = out_weight.shape[1]
    quarter = rows // lax.axis_size("y")
    half16, full32 = jnp.bfloat16, jnp.float32
    table = jnp.asarray(transform_table(rows))
    gain = lax.dynamic_slice(skip_gain, (ctx * share,), (share,))[:, None]

    with jax.named_scope("pack"):
        square = pltpu.VMEM((rows, channels), half16)
        outgoing, weight_half = whole(
            pack_kernel,
            [((ctx_count, 2 * share, rows), half16), ((channels // 2, features), half16)],
            [HBM] * 4,
            [HBM] * 2,
            [
                square,
                square,
                square,
                pltpu.VMEM((channels // 2, features), half16),
                pltpu.VMEM((ctx_count, 2 * share, rows), half16),
                pltpu.SemaphoreType.DMA((5 + 2 * PIECES,)),
            ],
            limit=60,
        )(key_branch, value_branch, filters, out_weight)
    with jax.named_scope("weights"):
        toward, back = mirrored(weight_half, 1), mirrored(weight_half, -1)
    arrived = lax.all_to_all(outgoing, ("block", "core"), split_axis=0, concat_axis=0, tiled=True)
    spec = pltpu.VMEM((ctx_count, share, 2 * rows), full32)
    with jax.named_scope("conv"):
        (total,) = whole(
            conv_kernel,
            [((ctx_count, share, rows), half16)],
            [VMEM] * 3,
            [VMEM],
            [spec] * 3,
            limit=24,
        )(arrived, gain, table)
    with jax.named_scope("weights"):
        total, toward = lax.optimization_barrier((total, toward))
        far = mirrored(toward, 1)
        swapped = [along_core(toward)]
    total = lax.all_to_all(total, ("block", "core"), split_axis=0, concat_axis=0, tiled=True)
    with jax.named_scope("weights"):
        total, far, back, *swapped = lax.optimization_barrier((total, far, back, *swapped))
        weights = (toward, along_core(back), back, swapped[0], far, along_core(far))
    with jax.named_scope("gate"):
        gated = whole(
            gate_kernel, [((quarter, channels), half16)] * 4, [VMEM] * 2, [VMEM] * 4, [square]
        )(total, query_branch)
    with jax.named_scope("quarters"):
        others = mirrored(gated[1], 1), mirrored(gated[2], -1), along_y(gated[3], 2)
    cost = quarter * channels * features
    with jax.named_scope("own"):
        (partial_value,) = whole(
            own_kernel, [((quarter, features), full32)], [VMEM] * 2, [VMEM], limit=12, cost=cost
        )(gated[0], out_weight)
    with jax.named_scope("rest"):
        width = features // STREAMS
        halves = [
            whole(
                functools.partial(rest_kernel, stream * width),
                [((quarter // 2, width), half16)] * 2,
                [VMEM] * (4 + len(weights)),
                [VMEM] * 2,
                limit=20,
                cost=cost,
            )(partial_value, *others, *weights)
            for stream in range(STREAMS)
        ]
    with jax.named_scope("gather"):
        return reduce_and_gather(halves, (rows, features))


def solution(mesh):
    fine = Mesh(mesh.devices.reshape(-1, 2, 4, 2), ("block", "core", "y", "z"))
    ctx, tp = ("block", "core"), ("y", "z")
    placed = (P(ctx, tp), P(ctx, tp), P(ctx, tp), P(ctx, tp), P(tp), P(tp, None))
    return jax.shard_map(
        body, mesh=fine, in_specs=placed, out_specs=P(ctx, None), check_vma=False
    )
```

```python
import functools
import math

import jax
import jax.numpy as jnp
import ml_dtypes
import numpy as np
from jax import lax
from jax.experimental import pallas as pl
from jax.experimental.pallas import tpu as pltpu
from jax.sharding import Mesh, PartitionSpec as P

MIB = 1024 * 1024
GROUP = 4
PIECES = 4
STREAMS = 2
WIDTH = 512


def transform_table(rows):
    j = np.arange(rows, dtype=np.int64)[:, None]
    f = np.arange(rows, dtype=np.int64)[None, :]
    angle = (j * (2 * f + 1) % (4 * rows)) * (2.0 * math.pi / (4 * rows))
    return np.concatenate([np.cos(angle), -np.sin(angle)], 1).astype(ml_dtypes.bfloat16)


def pack_kernel(
    key_hbm, value_hbm, filter_hbm, weight_hbm, out_hbm, half_hbm,
    key_ref, value_ref, filter_ref, half_ref, out_ref, sems,
):
    parts, both, rows = out_hbm.shape
    share, half = both // 2, half_hbm.shape[0]
    start = pl.multiple_of(lax.axis_index("core") * half, half)
    piece = half // PIECES
    moves = [(key_hbm, key_ref), (value_hbm, value_ref), (filter_hbm, filter_ref)]
    for i in range(PIECES):
        here = pl.ds(i * piece, piece)
        moves.append((weight_hbm.at[pl.ds(start + i * piece, piece)], half_ref.at[here]))
    arriving = [pltpu.make_async_copy(*move, sems.at[i]) for i, move in enumerate(moves)]
    leaving = []

    def send(source, target):
        leaving.append(pltpu.make_async_copy(source, target, sems.at[len(moves) + len(leaving)]))
        leaving[-1].start()

    for copy in arriving:
        copy.start()
    arriving[0].wait()
    arriving[1].wait()
    mixer = key_ref[...].astype(jnp.float32) * value_ref[...].astype(jnp.float32)
    out_ref[:, :share, :] = mixer.astype(jnp.bfloat16).T.reshape(parts, share, rows)
    send(out_ref.at[:, pl.ds(0, share)], out_hbm.at[:, pl.ds(0, share)])
    arriving[2].wait()
    out_ref[:, share:, :] = filter_ref[...].T.reshape(parts, share, rows)
    send(out_ref.at[:, pl.ds(share, share)], out_hbm.at[:, pl.ds(share, share)])
    for i in range(PIECES):
        arriving[3 + i].wait()
        here = pl.ds(i * piece, piece)
        send(half_ref.at[here], half_hbm.at[here])
    for copy in leaving:
        copy.wait()


def conv_kernel(signal_ref, gain_ref, table_ref, out_ref, mixer_spec, filter_spec, product):
    blocks, both, rows = signal_ref.shape
    share = both // 2
    table = table_ref[...]
    lane = lax.broadcasted_iota(jnp.int32, (8, 128), 1)
    sign = jnp.where(lane % 2 == 0, 1.0, -1.0).astype(jnp.float32)
    for part, spec in enumerate((mixer_spec, filter_spec)):
        flat = signal_ref[:, part * share : (part + 1) * share, :].reshape(blocks * share, rows)
        value = jnp.dot(flat, table, preferred_element_type=jnp.float32)
        spec[...] = value.reshape(blocks, share, 2 * rows)

    for column in range(0, rows, 128):
        real, imag = slice(column, column + 128), slice(rows + column, rows + column + 128)
        for row in range(0, share, 8):
            here = slice(row, row + 8)

            def load(ref, block):
                return ref[block, here, real], ref[block, here, imag]

            for block in reversed(range(1, blocks)):
                now_real, now_imag = load(mixer_spec, block)
                last_real, last_imag = load(mixer_spec, block - 1)
                mixer_spec[block, here, real] = now_real - sign * last_imag
                mixer_spec[block, here, imag] = now_imag + sign * last_real

            for first in range(0, blocks, GROUP):
                sums = [[None] * 3 for _ in range(GROUP)]
                held = {}
                for lag in range(first + GROUP):
                    filter_real, filter_imag = load(filter_spec, lag)
                    filter_both = filter_real + filter_imag
                    for i in range(GROUP):
                        block = first + i - lag
                        if block < 0:
                            continue
                        if block not in held:
                            real_part, imag_part = load(mixer_spec, block)
                            held[block] = (real_part, imag_part, real_part + imag_part)
                        terms = (
                            filter_real * held[block][0],
                            filter_imag * held[block][1],
                            filter_both * held[block][2],
                        )
                        for s in range(3):
                            sums[i][s] = terms[s] if sums[i][s] is None else sums[i][s] + terms[s]
                    held.pop(first + GROUP - 1 - lag, None)
                for i in range(GROUP):
                    one, two, three = sums[i]
                    product[first + i, here, real] = one - two
                    product[first + i, here, imag] = three - one - two

    flat = product[...].astype(jnp.bfloat16).reshape(blocks * share, 2 * rows)
    conv = lax.dot_general(
        flat, table, (((1,), (1,)), ((), ())), preferred_element_type=jnp.float32
    ) * (1.0 / rows)
    mixer = signal_ref[:, :share, :].astype(jnp.float32)
    total = conv.reshape(blocks, share, rows) + gain_ref[...] * mixer
    out_ref[...] = total.astype(jnp.bfloat16)


def gate_kernel(total_ref, query_ref, own_ref, toward_ref, back_ref, far_ref, gated_ref):
    rows, channels = query_ref.shape
    core, y, keep = lax.axis_index("core"), lax.axis_index("y"), lax.axis_index("z")
    total = total_ref[...].reshape(channels, rows).T.astype(jnp.float32)
    gated_ref[...] = (query_ref[...].astype(jnp.float32) * total).astype(jnp.bfloat16)
    half, piece = channels // 2, own_ref.shape[0] // 2
    steps = (own_ref, y), (toward_ref, y + 1 - 2 * core), (back_ref, y + 3 + 2 * core)
    for out_ref, place in steps + ((far_ref, y + 2),):
        for part, side in enumerate((1 - keep, keep)):
            start = pl.multiple_of((place % 4 * 2 + side) * piece, piece)
            rows_out = slice(part * piece, (part + 1) * piece)
            if out_ref is own_ref:
                out_ref[rows_out, :] = gated_ref[pl.ds(start, piece), :]
                continue
            for column, sender in enumerate((core, 1 - core)):
                columns = pl.ds(pl.multiple_of(sender * half, half), half)
                here = slice(column * half, (column + 1) * half)
                out_ref[rows_out, here] = gated_ref[pl.ds(start, piece), columns]


def own_kernel(gated_ref, weight_ref, out_ref):
    for start in range(0, out_ref.shape[1], WIDTH):
        columns = slice(start, start + WIDTH)
        out_ref[:, columns] = jnp.dot(
            gated_ref[...], weight_ref[:, columns], preferred_element_type=jnp.float32
        )


def rest_kernel(first, partial_ref, *refs):
    gated, weights, (other_ref, own_ref) = refs[:3], refs[3:-2], refs[-2:]
    piece, columns = other_ref.shape
    depth = weights[0].shape[0]
    for column in range(0, columns, WIDTH):
        here = slice(first + column, first + column + WIDTH)
        value = partial_ref[:, here]
        for i, weight in enumerate(weights):
            half = slice(i % 2 * depth, (i % 2 + 1) * depth)
            value = value + jnp.dot(
                gated[i // 2][:, half], weight[:, here], preferred_element_type=jnp.float32
            )
        value = value.astype(jnp.bfloat16)
        other_ref[:, column : column + WIDTH] = value[:piece]
        own_ref[:, column : column + WIDTH] = value[piece:]


def place_kernel(layout, fresh, *refs):
    pieces, (out_ref, sems) = refs[0 if fresh else 1 : -2], refs[-2:]
    y, z = lax.axis_index("y"), lax.axis_index("z")
    copies = []
    for i, (piece, (slot, column)) in enumerate(zip(pieces, layout)):
        count, width = piece.shape
        row = ((y + slot // 2) % 4 * 2 + (z + slot) % 2) * count
        target = out_ref.at[pl.ds(pl.multiple_of(row, count), count), pl.ds(column, width)]
        copies.append(pltpu.make_async_copy(piece, target, sems.at[i]))
    for copy in copies:
        copy.start()
    for copy in copies:
        copy.wait()


VMEM = pl.BlockSpec(memory_space=pltpu.VMEM)
HBM = pl.BlockSpec(memory_space=pltpu.HBM)


def whole(kernel, shapes, in_specs, out_specs, scratch=(), limit=16, cost=0, **rest):
    return pl.pallas_call(
        kernel,
        out_shape=[jax.ShapeDtypeStruct(*shape) for shape in shapes],
        in_specs=in_specs,
        out_specs=out_specs,
        scratch_shapes=list(scratch),
        compiler_params=pltpu.CompilerParams(vmem_limit_bytes=limit * MIB),
        cost_estimate=pl.CostEstimate(flops=2 * cost, bytes_accessed=8 * MIB, transcendentals=0),
        **rest,
    )


def place_pieces(out, shape, found):
    fresh = out is None
    layout, values = [item[:2] for item in found], [item[2] for item in found]
    return whole(
        functools.partial(place_kernel, layout, fresh),
        [(shape, jnp.bfloat16)],
        [HBM] * (not fresh) + [VMEM] * len(values),
        [HBM],
        [pltpu.SemaphoreType.DMA((len(values),))],
        input_output_aliases={} if fresh else {0: 0},
    )(*([] if fresh else [out]), *values)[0]


def swap(axis):
    return lambda value: lax.ppermute(value, axis, [(0, 1), (1, 0)])


along_z, along_core = swap("z"), swap("core")


def along_y(value, steps):
    count = lax.axis_size("y")
    return lax.ppermute(value, "y", [(i, (i + steps) % count) for i in range(count)])


def mirrored(value, steps):
    count = lax.axis_size("y")
    pairs = [
        (core * count + i, core * count + (i + (steps, -steps)[core]) % count)
        for core in range(2)
        for i in range(count)
    ]
    return lax.ppermute(value, ("core", "y"), pairs)


def add(*terms):
    return sum(term.astype(jnp.float32) for term in terms).astype(jnp.bfloat16)


def reduce_and_gather(halves, shape):
    first, last, early, late = [], [], [], []
    width = halves[0][1].shape[1]
    arrived = [along_z(other) for other, _ in halves]
    for (_, own), from_z in zip(halves, arrived):
        own = add(own, from_z)
        first.append((own, along_z(own), along_y(own, 1), along_y(own, -1)))
    for stream, (own, own_z, down, up) in enumerate(first):
        column = stream * width
        own_z, down, up = lax.optimization_barrier((own_z, down, up))
        early += [(slot, column, value) for slot, value in ((0, own), (1, own_z), (6, down), (2, up))]
        last.append((along_z(up), along_y(up, -1), along_y(own_z, 1)))
    out = place_pieces(None, shape, early)
    for stream, (up_z, far, down_z) in enumerate(last):
        column = stream * width
        up_z, far, down_z = lax.optimization_barrier((up_z, far, down_z))
        late += [(3, column, up_z), (4, column, far), (7, column, down_z)]
        middle = width // 2
        late.append((5, column, along_y(down_z[:, :middle], 1)))
        late.append((5, column + middle, along_y(up_z[:, middle:], -1)))
    return place_pieces(out, shape, late)


def body(query_branch, key_branch, value_branch, filters, skip_gain, out_weight):
    ctx = lax.axis_index("block") * 2 + lax.axis_index("core")
    ctx_count = lax.axis_size("block") * 2
    rows, channels = query_branch.shape
    share = channels // ctx_count
    features = out_weight.shape[1]
    quarter = rows // lax.axis_size("y")
    half16, full32 = jnp.bfloat16, jnp.float32
    table = jnp.asarray(transform_table(rows))
    gain = lax.dynamic_slice(skip_gain, (ctx * share,), (share,))[:, None]

    with jax.named_scope("pack"):
        square = pltpu.VMEM((rows, channels), half16)
        outgoing, weight_half = whole(
            pack_kernel,
            [((ctx_count, 2 * share, rows), half16), ((channels // 2, features), half16)],
            [HBM] * 4,
            [HBM] * 2,
            [
                square,
                square,
                square,
                pltpu.VMEM((channels // 2, features), half16),
                pltpu.VMEM((ctx_count, 2 * share, rows), half16),
                pltpu.SemaphoreType.DMA((5 + 2 * PIECES,)),
            ],
            limit=60,
        )(key_branch, value_branch, filters, out_weight)
    with jax.named_scope("weights"):
        toward, back = mirrored(weight_half, 1), mirrored(weight_half, -1)
    arrived = lax.all_to_all(outgoing, ("block", "core"), split_axis=0, concat_axis=0, tiled=True)
    spec = pltpu.VMEM((ctx_count, share, 2 * rows), full32)
    with jax.named_scope("conv"):
        (total,) = whole(
            conv_kernel,
            [((ctx_count, share, rows), half16)],
            [VMEM] * 3,
            [VMEM],
            [spec] * 3,
            limit=24,
        )(arrived, gain, table)
    with jax.named_scope("weights"):
        total, toward = lax.optimization_barrier((total, toward))
        far = mirrored(toward, 1)
        swapped = [along_core(toward)]
    total = lax.all_to_all(total, ("block", "core"), split_axis=0, concat_axis=0, tiled=True)
    with jax.named_scope("weights"):
        total, *swapped = lax.optimization_barrier((total, *swapped))
    with jax.named_scope("gate"):
        gated = list(whole(
            gate_kernel, [((quarter, channels), half16)] * 4, [VMEM] * 2, [VMEM] * 4, [square]
        )(total, query_branch))
    with jax.named_scope("quarters"):
        others = mirrored(gated[1], 1), mirrored(gated[2], -1), along_y(gated[3], 2)
    with jax.named_scope("weights"):
        swapped_back = along_core(back)
        gated[0], far = lax.optimization_barrier((gated[0], far))
        weights = (toward, swapped_back, back, swapped[0], far, along_core(far))
    cost = quarter * channels * features
    with jax.named_scope("own"):
        (partial_value,) = whole(
            own_kernel, [((quarter, features), full32)], [VMEM] * 2, [VMEM], limit=12, cost=cost
        )(gated[0], out_weight)
    with jax.named_scope("rest"):
        width = features // STREAMS
        halves = [
            whole(
                functools.partial(rest_kernel, stream * width),
                [((quarter // 2, width), half16)] * 2,
                [VMEM] * (4 + len(weights)),
                [VMEM] * 2,
                limit=20,
                cost=cost,
            )(partial_value, *others, *weights)
            for stream in range(STREAMS)
        ]
    with jax.named_scope("gather"):
        return reduce_and_gather(halves, (rows, features))


def solution(mesh):
    fine = Mesh(mesh.devices.reshape(-1, 2, 4, 2), ("block", "core", "y", "z"))
    ctx, tp = ("block", "core"), ("y", "z")
    placed = (P(ctx, tp), P(ctx, tp), P(ctx, tp), P(ctx, tp), P(tp), P(tp, None))
    return jax.shard_map(
        body, mesh=fine, in_specs=placed, out_specs=P(ctx, None), check_vma=False
    )
```
